128 devices in a mesh: gx: 4 (over x), gy: 4 (over y), gz: 8 (over z, core).
Axes of the slice: x: 4, y: 4, z: 4, core: 2. Of those that a mesh axis runs over, the one named last changes fastest.
Arguments:
- source_term: float32 [32, 128, 1024], P('gx', 'gy', 'gz'), may hold values from -8 to 8
- conductivity: float32 [32, 128, 1024], P('gx', 'gy', 'gz'), may hold values from 0.3 to 3
- jacobi_weights: float32 [3], replicated, may hold values from 0.7 to 0.95
- cotangent: float32 [32, 128, 1024], P('gx', 'gy', 'gz'), may hold values from -4 to 4
Outputs:
- solution: float32 [32, 128, 1024], P('gx', 'gy', 'gz')
- source_grad: float32 [32, 128, 1024], P('gx', 'gy', 'gz')
- weight_grad: float32 [3], replicated
The draws below stay inside these ranges and needn't reach their ends.
All inputs are finite; a program needn't handle non-finite values.
Results may differ from the reference program's by a relative error of at most 0.0001.
Values sent between devices are 32-bit elements; how exact they have to be, the bound alone decides.
A program may use at most 128 MiB of HBM per device.

```python
import math
import jax
import jax.numpy as jnp
from jax import lax

LEVELS = 3
SWEEPS = 2
COARSE_SWEEPS = 8
CYCLES = 2
NX = 32
NY = 128
NZ = 1024


def smooth_wave(key):
    freq_key, phase_key = jax.random.split(key)
    freqs = jax.random.uniform(freq_key, (3, 3), jnp.float32, 0.3, 1.2)
    phases = jax.random.uniform(phase_key, (3,), jnp.float32, 0.0, 2.0 * math.pi)
    first = ((jnp.arange(NX, dtype=jnp.float32) + 0.5) / NX)[:, None, None]
    second = ((jnp.arange(NY, dtype=jnp.float32) + 0.5) / NY)[None, :, None]
    third = ((jnp.arange(NZ, dtype=jnp.float32) + 0.5) / NZ)[None, None, :]
    total = jnp.zeros((NX, NY, NZ), jnp.float32)
    for term in range(3):
        angle_now = 2.0 * math.pi * (freqs[term, 0] * first + freqs[term, 1] * second + freqs[term, 2] * third) + phases[term]
        total = total + jnp.cos(angle_now) / 3.0
    return total


def draw_source_term(key, part):
    key = jax.random.fold_in(key, 5)
    wave_key, rough_key = jax.random.split(key)
    wave = smooth_wave(wave_key)
    rough = jnp.clip(jax.random.normal(rough_key, (NX, NY, NZ), jnp.float32), -4.0, 4.0)
    values = rough + 1.0 + 0.5 * wave
    return values.astype(jnp.float32)


def draw_cotangent(key, part):
    key = jax.random.fold_in(key, 17)
    wave_key, rough_key = jax.random.split(key)
    wave = smooth_wave(wave_key)
    rough = 0.8 * jnp.clip(jax.random.normal(rough_key, (NX, NY, NZ), jnp.float32), -3.0, 3.0)
    values = rough + 0.6 + 0.3 * wave
    return values.astype(jnp.float32)


def draw_conductivity(key, part):
    key = jax.random.fold_in(key, 29)
    column_key, rough_key = jax.random.split(key)
    block = 2 ** (LEVELS - 1)
    columns = jax.random.bernoulli(column_key, 0.3, (NX // block, NY // block)).astype(jnp.float32)
    columns = jnp.repeat(jnp.repeat(columns, block, axis=0), block, axis=1)[:, :, None]
    rough = jax.random.uniform(rough_key, (NX, NY, NZ), jnp.float32, 0.0, 1.0)
    exponent = 0.6 * columns + 0.4 * rough
    return (0.3 * jnp.exp(exponent * math.log(10.0))).astype(jnp.float32)


def setup_inputs(seed: int = 0) -> dict:
    arg_keys = jax.random.split(jax.random.key(seed), 5)
    return {
        "source_term": draw_source_term(jax.random.fold_in(arg_keys[4], 71), 0),
        "conductivity": draw_conductivity(jax.random.fold_in(arg_keys[4], 71), 0),
        "jacobi_weights": jnp.clip(jax.random.uniform(arg_keys[2], (LEVELS,), jnp.float32, 0.7, 0.95), 0.7, 0.95),
        "cotangent": draw_cotangent(jax.random.fold_in(arg_keys[4], 71), 0),
    }


def neighbours(padded):
    return [padded[2:, 1:-1, 1:-1], padded[:-2, 1:-1, 1:-1], padded[1:-1, 2:, 1:-1], padded[1:-1, :-2, 1:-1], padded[1:-1, 1:-1, 2:], padded[1:-1, 1:-1, :-2]]

def coarsen(values):
    blocks = values.reshape(values.shape[0] // 2, 2, values.shape[1] // 2, 2, values.shape[2] // 2, 2)
    return lax.optimization_barrier(jnp.sum(blocks, axis=(1, 3, 5))) * 0.125

def refine(values):
    return jnp.repeat(jnp.repeat(jnp.repeat(values, 2, axis=0), 2, axis=1), 2, axis=2)

def build_section(coefficient, padded, factor):
    couplings = [factor * 0.5 * (coefficient + beside) for beside in neighbours(padded)]
    diagonal = couplings[0] + couplings[1] + couplings[2] + couplings[3] + couplings[4] + couplings[5]
    return (couplings, diagonal, 1.0 / diagonal)

def operate(current, section):
    couplings, diagonal, inverse = section
    beside = neighbours(jnp.pad(current, 1))
    summed = couplings[0] * beside[0]
    for direction in range(1, 6):
        summed = summed + couplings[direction] * beside[direction]
    return diagonal * current - summed

def smooth(current, source, section, weight, sweeps_count):
    for sweep_index in range(sweeps_count):
        defect = section[2] * (source - operate(current, section))
        current = current + weight * defect
    return current

def vcycle(current, source, sections, weights, level_index):
    section = sections[level_index]
    if level_index == LEVELS - 1:
        return smooth(jnp.zeros_like(source), source, section, weights[level_index], COARSE_SWEEPS)
    current = smooth(current, source, section, weights[level_index], SWEEPS)
    defect = source - operate(current, section)
    coarse_source = coarsen(defect)
    correction = vcycle(jnp.zeros_like(coarse_source), coarse_source, sections, weights, level_index + 1)
    current = current + refine(correction)
    return smooth(current, source, section, weights[level_index], SWEEPS)

def reference(source_term, conductivity, jacobi_weights, cotangent):
    sections = []
    coefficient = conductivity
    for level_index in range(LEVELS):
        sections.append(build_section(coefficient, jnp.pad(coefficient, 1), 0.25 ** level_index))
        coefficient = coarsen(coefficient)

    def solve(source, weights):
        current = jnp.zeros_like(source)
        for cycle_index in range(CYCLES):
            current = vcycle(current, source, sections, weights, 0)
        return current
    solution, pullback = jax.vjp(solve, source_term, jacobi_weights)
    source_grad, weight_grad = pullback(cotangent)
    return (solution, source_grad, weight_grad / (NX * NY * NZ))
```

```python
import functools

import jax
import jax.numpy as jnp
from jax import lax
from jax.experimental import pallas as pl
from jax.experimental.pallas import tpu as pltpu
from jax.sharding import PartitionSpec as P

MESH = pl.DeviceIdType.MESH
CELLS = 32 * 128 * 1024
PLANES = (16, 4, 2)
WORK = (48, 32, 24)
ROWS = (64, 48, 40)
GROUP = (64, 32, 32)
OWN = (32, 16, 8)
FIRST = (16, 8, 12)
AROUND = [(ds, dy) for ds in (-1, 0, 1) for dy in (-1, 0, 1) if (ds, dy) != (0, 0)]


def lane_of(rows):
    return lax.broadcasted_iota(jnp.int32, (rows, 128), 1)


def row_of(rows):
    return lax.broadcasted_iota(jnp.int32, (rows, 128), 0)


def roll(values, shift):
    shift = shift % 128
    return values if shift == 0 else pltpu.roll(values, shift, 1)


def kernel(
    f_ref, c_ref, w_ref, g_ref, sol_ref, grad_ref, wg_ref,
    pk, tb, ef, ua, ub, fr, kk, dd, qq, tt, sv,
    c1, ua1, ub1, fr1, kk1, dd1, qq1, tt1, sv1,
    c2, ua2, ub2, fr2, kk2, dd2, qq2, sv2,
    inside0, inside1, inside2, mats,
    *rest,
):
    ex = [rest[6 * i : 6 * i + 6] for i in range(5)]
    rest = rest[30:]
    ga = [rest[2 * i : 2 * i + 2] for i in range(3)]
    po, ob, ra, rb, rc = rest[6:11]
    send_sem, recv_sem = rest[11:13]

    x, y, z = lax.axis_index("gx"), lax.axis_index("gy"), lax.axis_index("gz")
    odd = lax.rem(z, 2)

    def flip(value, parity):
        return value + parity * (3 - 2 * value)

    part = flip(x, odd)
    slab = 4 * z + part

    def peer(ds, dy):
        other = lax.rem(slab + ds + 32, 32)
        oz = lax.div(other, 4)
        ox = flip(lax.rem(other, 4), lax.rem(oz, 2))
        return (ox, lax.rem(y + dy + 4, 4), oz)

    x_peers = [(lax.rem(x + d, 4), y, z) for d in (1, 2, 3)]
    y_peers = [(x, lax.rem(y + d, 4), z) for d in (1, 2, 3)]
    z_peers = [(x, y, lax.rem(z + d, 8)) for d in range(1, 8)]
    peers = {o: peer(*o) for o in AROUND}

    barrier = pltpu.get_barrier_semaphore()
    greeted = x_peers + list(peers.values()) + [y_peers[1]] + z_peers
    for device in greeted:
        pl.semaphore_signal(barrier, inc=1, device_id=device, device_id_type=MESH)

    pending = []
    counter = [0]

    def remote(src, dst, device):
        slot = counter[0]
        counter[0] += 1
        copy = pltpu.make_async_remote_copy(
            src_ref=src, dst_ref=dst, send_sem=send_sem.at[slot], recv_sem=recv_sem.at[slot],
            device_id=device, device_id_type=MESH,
        )
        copy.start()
        pending.append(copy)
        return copy

    lane32 = lane_of(32)
    for field, ref in enumerate((c_ref, f_ref, g_ref)):
        for x1 in range(2):
            planes = [ref[4 * x1 + x0] for x0 in range(4)]
            for p in range(4):
                packed = roll(planes[0], -32 * p)
                for x0 in range(1, 4):
                    packed = jnp.where(lane32 // 32 == x0, roll(planes[x0], 32 * (x0 - p)), packed)
                pk[p, field, x1] = packed
    pl.semaphore_wait(barrier, len(greeted))
    copies = []
    for d in (1, 2, 3):
        other = lax.rem(x + d, 4)
        copies.append(remote(pk.at[flip(other, odd)], tb.at[x], (other, y, z)))

    for level, ref in enumerate((inside0, inside1, inside2)):
        rows, lanes = row_of(WORK[level]) - 8, lane_of(WORK[level]) % GROUP[level] - FIRST[level]
        own = OWN[level]
        good = (lanes >= -8) & (lanes < own + 8)
        good &= ((rows >= 0) | (y > 0)) & ((rows < own) | (y < 3))
        good &= ((lanes >= 0) | (slab > 0)) & ((lanes < own) | (slab < 31))
        ref[...] = good.astype(jnp.float32)
    src, dst = row_of(128), lane_of(128)
    for t in range(2):
        mats[t] = jnp.where(dst == (2 * (src // 64) + t) * 32 + (src % 64) // 2, 0.125, 0.0)
        mats[2 + t] = jnp.where(src == (2 * (dst // 64) + t) * 32 + (dst % 64) // 2, 1.0, 0.0)
    mats[4] = jnp.where((dst // 32 == src // 32) & (dst % 32 == 8 + (src % 32) // 2), 0.125, 0.0)
    mats[5] = jnp.where((dst // 32 == src // 32) & (src % 32 == 8 + (dst % 32) // 2), 1.0, 0.0)
    for ref in (c1, ua1, ub1, tt1, c2, ua2, ub2):
        ref[...] = jnp.zeros_like(ref)
    for ref in (tt, ua, ub, ef):
        edge = jnp.zeros(ref.shape[:-2] + (8, 128), jnp.float32)
        ref[..., 0:8, :] = edge
        ref[..., 56:64, :] = edge

    tb[x] = pk[part]
    for copy in copies:
        copy.wait_recv()

    group32 = lane32 // 64

    def build(field, unused):
        for h in range(2):
            for x1 in range(2):
                low, high = tb[h, field, x1], tb[2 + h, field, x1]
                for x0 in range(4):
                    plane = jnp.where(group32 == 0, roll(low, 16 - 32 * x0), roll(high, 80 - 32 * x0))
                    ef[field, 1 + 8 * h + 4 * x1 + x0, 16:48] = plane
        return unused

    lax.fori_loop(0, 3, build, 0)

    def pack(level, ref, bufs, count):
        zs, ys = bufs[:2]
        own, first, group = OWN[level], FIRST[level], GROUP[level]
        per = group // 8
        lanes = lane_of(own) % group
        lanes8 = lane_of(8) % group
        mine = (lanes8 >= first) & (lanes8 < first + own)

        def step(field, unused):
            for i in range(PLANES[level] // per):
                left = right = None
                for k in range(per):
                    plane = ref[field, 1 + i * per + k, 16 : 16 + own]
                    a, b = roll(plane, 8 * k - first), roll(plane, 8 * k - first - own + 8)
                    left = a if k == 0 else jnp.where(lanes // 8 == k, a, left)
                    right = b if k == 0 else jnp.where(lanes // 8 == k, b, right)
                zs[0, field, i] = left
                zs[1, field, i] = right
            for i in range(PLANES[level] // 2):
                for side, at in ((0, 16), (1, 8 + own)):
                    a, b = ref[field, 1 + 2 * i, at : at + 8], ref[field, 2 + 2 * i, at : at + 8]
                    ys[side, field, i] = jnp.where(mine, a, roll(b, group // 2))
            return unused

        lax.fori_loop(0, count, step, 0)

    def send(level, bufs):
        zs, ys, ls, rs, yl, yh = bufs
        own = OWN[level]
        low, high, face = pl.ds(0, 8), pl.ds(own + 8, 8), pl.ds(8, own)
        first, last = pl.ds(0, 8), pl.ds(own - 8, 8)
        return [
            remote(zs.at[1], ls.at[:, :, face], peers[1, 0]),
            remote(zs.at[0], rs.at[:, :, face], peers[-1, 0]),
            remote(ys.at[1], yl, peers[0, 1]),
            remote(ys.at[0], yh, peers[0, -1]),
            remote(zs.at[1, :, :, last], ls.at[:, :, low], peers[1, 1]),
            remote(zs.at[1, :, :, first], ls.at[:, :, high], peers[1, -1]),
            remote(zs.at[0, :, :, last], rs.at[:, :, low], peers[-1, 1]),
            remote(zs.at[0, :, :, first], rs.at[:, :, high], peers[-1, -1]),
        ]

    def ghosts(level, ref, count):
        planes, work, group = PLANES[level], WORK[level], GROUP[level]
        at = slice(8, 8 + work)
        lanes = lane_of(work)
        for field in range(count):
            before, after = ref[field, planes, at], ref[field, 1, at]
            ref[field, 0, at] = jnp.where(lanes < group, 0.0, roll(before, group))
            ref[field, planes + 1, at] = jnp.where(lanes >= 128 - group, 0.0, roll(after, -group))

    insides = (inside0, inside1, inside2)

    def unpack(level, ref, bufs, count):
        ls, rs, yl, yh = bufs[2:]
        own, first, group, work = OWN[level], FIRST[level], GROUP[level], WORK[level]
        per = group // 8
        lanes = lane_of(work) % group
        mine = (lanes >= first) & (lanes < first + own)
        before = lanes < first

        def step(field, unused):
            keep = insides[level][...]
            for i in range(PLANES[level] // per):
                left, right = ls[field, i], rs[field, i]
                for k in range(per):
                    plane = i * per + k
                    low, high = yl[field, plane // 2], yh[field, plane // 2]
                    if plane % 2:
                        low, high = roll(low, -(group // 2)), roll(high, -(group // 2))
                    middle = ref[field, 1 + plane, 16 : 16 + own]
                    base = jnp.concatenate([low, middle, high], axis=0)
                    sides = jnp.where(
                        before, roll(left, first - 8 - 8 * k), roll(right, first + own - 8 * k)
                    )
                    ref[field, 1 + plane, 8 : 8 + work] = jnp.where(mine, base, sides) * keep
            return unused

        lax.fori_loop(0, count, step, 0)

    def beside(ref, field, plane, work):
        here = ref[field, plane + 1, 8 : 8 + work]
        return here, [
            ref[field, plane + 2, 8 : 8 + work],
            ref[field, plane, 8 : 8 + work],
            ref[field, plane + 1, 9 : 9 + work],
            ref[field, plane + 1, 7 : 7 + work],
            roll(here, -1),
            roll(here, 1),
        ]

    def setup(level, cells, kref, dref, qref):
        work = WORK[level]
        factor = 0.5 * 0.25**level

        def step(plane, unused):
            here, around = beside(cells, 0, plane, work)
            couplings = [factor * (here + other) for other in around]
            diagonal = couplings[0]
            for coupling in couplings[1:]:
                diagonal = diagonal + coupling
            good = (insides[level][...] > 0.5) & (diagonal > 0.0)
            inverse = jnp.where(good, 1.0 / jnp.where(good, diagonal, 1.0), 0.0)
            for index, coupling in enumerate(couplings):
                kref[index, plane] = inverse * coupling
            dref[plane] = diagonal
            qref[plane] = inverse
            return unused

        lax.fori_loop(0, PLANES[level], step, 0)

    krefs, drefs, frefs, svs = (kk, kk1, kk2), (dd, dd1, dd2), (fr, fr1, fr2), (sv, sv1, sv2)

    def residual(level, ref, field, plane):
        here, around = beside(ref, field, plane, WORK[level])
        total = frefs[level][field, plane] - here
        for index in range(6):
            total = total + krefs[level][index, plane] * around[index]
        return here, total

    def sweep(level, old, new, save=None):
        weight = w_ref[level]

        def step(plane, unused):
            for field in range(2):
                here, r = residual(level, old, field, plane)
                new[field, plane + 1, 8 : 8 + WORK[level]] = here + weight * r
                if save is not None:
                    svs[level][save, field, plane] = r[8 : 8 + OWN[level]]
            return unused

        lax.fori_loop(0, PLANES[level], step, 0)
        ghosts(level, new, 2)

    def first_sweep(level, new):
        weight = w_ref[level]

        def step(plane, unused):
            for field in range(2):
                new[field, plane + 1, 8 : 8 + WORK[level]] = weight * frefs[level][field, plane]
            return unused

        lax.fori_loop(0, PLANES[level], step, 0)
        ghosts(level, new, 2)

    def defect(level, ref, out):
        work = WORK[level]

        def step(pair, unused):
            for field in range(2):
                total = None
                for side in range(2):
                    plane = 2 * pair + side
                    e = drefs[level][plane] * residual(level, ref, field, plane)[1]
                    total = e if total is None else total + e
                out[field, pair, 8 : 8 + work] = total
            return unused

        lax.fori_loop(0, PLANES[level] // 2, step, 0)

    def dot(a, b):
        return jnp.dot(a, b, precision=lax.Precision.HIGHEST, preferred_element_type=jnp.float32)

    def pairs(ref, field, plane, rows):
        even = ref[field, plane, pl.ds(0, rows // 2, stride=2), :]
        return even + ref[field, plane, pl.ds(1, rows // 2, stride=2), :]

    def restricted(level, ref, field):
        if level == 0:
            a = jnp.concatenate([pairs(ref, field, m, 64) for m in range(4)], axis=0)
            b = jnp.concatenate([pairs(ref, field, 4 + m, 64) for m in range(4)], axis=0)
            return (dot(a, mats[0]) + dot(b, mats[1])).reshape(4, 32, 128)
        a = jnp.concatenate([pairs(ref, field, m, 48) for m in range(2)], axis=0)
        return dot(a, mats[4]).reshape(2, 24, 128)

    def prolong(level, ref, out):
        for field in range(2):
            if level == 0:
                w = ref[field, 1:5, 8:40].reshape(128, 128)
                for t in range(2):
                    moved = dot(w, mats[2 + t]).reshape(4, 32, 128)
                    for m in range(4):
                        out[field, 4 * t + m, pl.ds(0, 32, stride=2), :] = moved[m]
                        out[field, 4 * t + m, pl.ds(1, 32, stride=2), :] = moved[m]
            else:
                w = ref[field, 1:3, 8:32].reshape(48, 128)
                moved = dot(w, mats[5]).reshape(2, 24, 128)
                for m in range(2):
                    out[field, m, pl.ds(0, 24, stride=2), :] = moved[m]
                    out[field, m, pl.ds(1, 24, stride=2), :] = moved[m]

    def product(level, a, b, fa, fb):
        own, first = OWN[level], FIRST[level]
        lanes = lane_of(own) % GROUP[level]
        mine = (lanes >= first) & (lanes < first + own)

        def step(plane, total):
            saved = svs[level]
            value = drefs[level][plane, 8 : 8 + own] * saved[a, fa, plane] * saved[b, fb, plane]
            value = jnp.where(mine, value, 0.0)
            for tile in range(own // 8):
                total = total + value[8 * tile : 8 * tile + 8]
            return total

        return lax.fori_loop(0, PLANES[level], step, jnp.zeros((8, 128), jnp.float32))

    def gather(bufs):
        own, land = bufs
        return [
            remote(own, land.at[1 - ds, :, :, pl.ds(8 - 8 * dy, 8)], peers[ds, dy])
            for ds, dy in AROUND
        ]

    lanes2 = lane_of(24) % 32

    def gathered(land, field, plane):
        sides = jnp.where(
            lanes2 < 12, roll(land[0, field, plane], -8), roll(land[2, field, plane], 8)
        )
        mine = (lanes2 >= 12) & (lanes2 < 20)
        return jnp.where(mine, land[1, field, plane], sides) * inside2[...]

    pack(0, ef, ex[0], 3)
    copies = send(0, ex[0])

    def add_planes(pair, unused):
        tt[0, pair, 16:48] = ef[0, 1 + 2 * pair, 16:48] + ef[0, 2 + 2 * pair, 16:48]
        return unused

    lax.fori_loop(0, 8, add_planes, 0)
    early = restricted(0, tt, 0)
    for pair in range(2):
        tt1[0, pair, 8:40] = early[2 * pair] + early[2 * pair + 1]
    early = restricted(1, tt1, 0)
    own2, land2 = ga[0]
    for plane in range(2):
        own2[0, plane] = early[plane, 8:16]
        land2[1, 0, plane, 8:16] = early[plane, 8:16]
    coarse_copies = gather(ga[0])

    for copy in copies:
        copy.wait_recv()
    unpack(0, ef, ex[0], 3)
    ghosts(0, ef, 1)
    setup(0, ef, kk, dd, qq)

    def right_side(plane, unused):
        for field in range(2):
            fr[field, plane] = qq[plane] * ef[1 + field, plane + 1, 8:56]
        return unused

    lax.fori_loop(0, 16, right_side, 0)

    first_sweep(0, ua)
    sweep(0, ua, ub, 0)
    defect(0, ub, tt)

    def coarse_right_side(level, source, fine):
        for field in range(2):
            values = restricted(level, fine, field)
            for plane in range(PLANES[level + 1]):
                source(field, plane, values[plane])

    def keep1(field, plane, value):
        fr1[field, plane] = value

    coarse_right_side(0, keep1, tt)

    def add_planes_whole(pair, unused):
        tt[0, pair, 8:56] = ef[0, 1 + 2 * pair, 8:56] + ef[0, 2 + 2 * pair, 8:56]
        return unused

    lax.fori_loop(0, 8, add_planes_whole, 0)
    cells = restricted(0, tt, 0)
    for plane in range(4):
        c1[0, plane + 1, 8:40] = cells[plane] * inside1[...]
    ghosts(1, c1, 1)
    setup(1, c1, kk1, dd1, qq1)
    for copy in coarse_copies:
        copy.wait_recv()
    for plane in range(2):
        c2[0, plane + 1, 8:32] = gathered(land2, 0, plane)
    ghosts(2, c2, 1)
    setup(2, c2, kk2, dd2, qq2)

    def scale1():
        for field in range(2):
            for plane in range(4):
                fr1[field, plane] = qq1[plane] * fr1[field, plane]

    def middle(cycle):
        first_sweep(1, ua1)
        sweep(1, ua1, ub1, 2 * cycle)
        defect(1, ub1, tt1)
        own, land = ga[1 + cycle]

        def keep2(field, plane, value):
            scaled = qq2[plane, 8:16] * value[8:16]
            own[field, plane] = scaled
            land[1, field, plane, 8:16] = scaled

        coarse_right_side(1, keep2, tt1)
        copies = gather(ga[1 + cycle])
        if cycle == 0:
            pack(1, ub1, ex[1], 2)
            more = send(1, ex[1])
        for copy in copies:
            copy.wait_recv()
        for field in range(2):
            for plane in range(2):
                fr2[field, plane] = gathered(land, field, plane)
        first_sweep(2, ua2)
        refs = (ua2, ub2)
        for index in range(1, 8):
            save = cycle if index == 3 + cycle else None
            sweep(2, refs[(index + 1) % 2], refs[index % 2], save)
        prolong(1, ub2, tt1)
        if cycle == 0:
            for copy in more:
                copy.wait_recv()
            unpack(1, ub1, ex[1], 2)
        for field in range(2):
            for plane in range(4):
                ub1[field, plane + 1, 8:40] = (
                    ub1[field, plane + 1, 8:40] + tt1[field, plane // 2, 8:40]
                )
        ghosts(1, ub1, 2)
        sweep(1, ub1, ua1, 1 + 2 * cycle)
        sweep(1, ua1, ub1)

    def correct(ref):
        prolong(0, ub1, tt)

        def step(plane, unused):
            for field in range(2):
                ref[field, plane + 1, 16:48] = (
                    ref[field, plane + 1, 16:48] + tt[field, lax.div(plane, 2), 16:48]
                )
            return unused

        lax.fori_loop(0, 16, step, 0)

    def fine_halo(ref, bufs):
        pack(0, ref, bufs, 2)
        for copy in send(0, bufs):
            copy.wait_recv()
        unpack(0, ref, bufs, 2)
        ghosts(0, ref, 2)

    scale1()
    middle(0)
    correct(ub)
    fine_halo(ub, ex[2])
    sweep(0, ub, ua)
    sweep(0, ua, ub, 1)
    sweep(0, ub, ua, 2)
    sweep(0, ua, ub)
    defect(0, ub, tt)

    def keep_c1(field, plane, value):
        ua1[field, plane + 1, 8:40] = value

    coarse_right_side(0, keep_c1, tt)
    pack(1, ua1, ex[3], 2)
    for copy in send(1, ex[3]):
        copy.wait_recv()
    unpack(1, ua1, ex[3], 2)
    for field in range(2):
        for plane in range(4):
            fr1[field, plane] = qq1[plane] * ua1[field, plane + 1, 8:40]
    middle(1)
    correct(ub)
    fine_halo(ub, ex[4])
    sweep(0, ub, ua, 3)

    scale = 1.0 / CELLS
    sums = [
        2.0 * (product(0, 0, 3, 0, 1) + product(0, 3, 0, 0, 1)) + 4.0 * product(0, 1, 2, 0, 1),
        16.0
        * (
            product(1, 0, 3, 0, 1)
            + product(1, 3, 0, 0, 1)
            + product(1, 1, 2, 0, 1)
            + product(1, 2, 1, 0, 1)
        ),
        512.0 * (product(2, 0, 1, 0, 1) + product(2, 1, 0, 0, 1)),
    ]
    for level in range(3):
        ra[z, 8 * level : 8 * level + 8] = sums[level] * scale
    copies_a = [remote(ra.at[z], ra.at[z], device) for device in z_peers]

    sweep(0, ua, ub)

    def leave(field, unused):
        for h in range(2):
            for x1 in range(2):
                planes = [ub[field, 1 + 8 * h + 4 * x1 + x0, 16:48] for x0 in range(4)]
                for g in range(2):
                    packed = roll(planes[0], -64 * g - 16)
                    for x0 in range(1, 4):
                        packed = jnp.where(
                            lane32 // 32 == x0, roll(planes[x0], 32 * x0 - 64 * g - 16), packed
                        )
                    po[2 * g + h, field, x1] = packed
        return unused

    lax.fori_loop(0, 2, leave, 0)
    copies_o = []
    for d in (1, 2, 3):
        other = lax.rem(x + d, 4)
        copies_o.append(remote(po.at[other], ob.at[part], (other, y, z)))
    ob[part] = po[x]

    for copy in copies_a:
        copy.wait_recv()
    total = ra[0]
    for index in range(1, 8):
        total = total + ra[index]
    rb[y] = total
    copies_b = [remote(rb.at[y], rb.at[y], device) for device in y_peers]

    for copy in copies_o:
        copy.wait_recv()
    for field, ref in enumerate((sol_ref, grad_ref)):
        for x1 in range(2):
            quarters = [ob[p, field, x1] for p in range(4)]
            for x0 in range(4):
                out = roll(quarters[0], -32 * x0)
                for p in range(1, 4):
                    out = jnp.where(lane32 // 32 == p, roll(quarters[p], 32 * (p - x0)), out)
                ref[4 * x1 + x0] = out

    for copy in copies_b:
        copy.wait_recv()
    total = rb[0]
    for index in range(1, 4):
        total = total + rb[index]
    rc[x] = total
    copies_c = [remote(rc.at[x], rc.at[x], device) for device in x_peers]
    for copy in copies_c:
        copy.wait_recv()
    total = rc[0]
    for index in range(1, 4):
        total = total + rc[index]
    for level in range(3):
        wg_ref[level] = jnp.sum(total[8 * level : 8 * level + 8])
    for copy in pending:
        copy.wait_send()


def f32(*shape):
    return pltpu.VMEM(shape, jnp.float32)


def exchange_buffers(level, count):
    own, strips, half = OWN[level], PLANES[level] * 8 // GROUP[level], PLANES[level] // 2
    return [
        f32(2, count, strips, own, 128),
        f32(2, count, half, 8, 128),
        f32(count, strips, own + 16, 128),
        f32(count, strips, own + 16, 128),
        f32(count, half, 8, 128),
        f32(count, half, 8, 128),
    ]


def level_buffers(level):
    planes, work, rows, own = PLANES[level], WORK[level], ROWS[level], OWN[level]
    out = [
        f32(2, planes + 2, rows, 128),
        f32(2, planes + 2, rows, 128),
        f32(2, planes, work, 128),
        f32(6, planes, work, 128),
        f32(planes, work, 128),
        f32(planes, work, 128),
    ]
    if level < 2:
        out.append(f32(2, planes // 2, rows, 128))
    out.append(f32(4 if level < 2 else 2, 2, planes, own, 128))
    return out


def body(source_term, conductivity, jacobi_weights, cotangent):
    scratch = [f32(4, 3, 2, 32, 128), f32(4, 3, 2, 32, 128), f32(3, 18, 64, 128)]
    scratch += level_buffers(0)
    scratch += [f32(1, 6, 48, 128)] + level_buffers(1)
    scratch += [f32(1, 4, 40, 128)] + level_buffers(2)
    scratch += [f32(WORK[level], 128) for level in range(3)] + [f32(6, 128, 128)]
    for level, count in ((0, 3), (1, 2), (0, 2), (1, 2), (0, 2)):
        scratch += exchange_buffers(level, count)
    for count in (1, 2, 2):
        scratch += [f32(count, 2, 8, 128), f32(3, count, 2, 24, 128)]
    scratch += [f32(4, 2, 2, 32, 128), f32(4, 2, 2, 32, 128)]
    scratch += [f32(8, 24, 128), f32(4, 24, 128), f32(4, 24, 128)]
    copies = 3 + 8 * 8 + 3 + 13
    scratch += [pltpu.SemaphoreType.DMA((copies,)), pltpu.SemaphoreType.DMA((copies,))]
    vmem = pl.BlockSpec(memory_space=pltpu.VMEM)
    smem = pl.BlockSpec(memory_space=pltpu.SMEM)
    block = jax.ShapeDtypeStruct(source_term.shape, jnp.float32)
    return pl.pallas_call(
        kernel,
        out_shape=(block, block, jax.ShapeDtypeStruct((3,), jnp.float32)),
        in_specs=[vmem, vmem, smem, vmem],
        out_specs=(vmem, vmem, smem),
        scratch_shapes=scratch,
        compiler_params=pltpu.CompilerParams(
            collective_id=0, has_side_effects=True, vmem_limit_bytes=48 * 2**20
        ),
    )(source_term, conductivity, jacobi_weights, cotangent)


def solution(mesh):
    return jax.shard_map(
        body,
        mesh=mesh,
        in_specs=(P("gx", "gy", "gz"), P("gx", "gy", "gz"), P(), P("gx", "gy", "gz")),
        out_specs=(P("gx", "gy", "gz"), P("gx", "gy", "gz"), P()),
        check_vma=False,
    )
```

```python
import functools

import jax
import jax.numpy as jnp
from jax import lax
from jax.experimental import pallas as pl
from jax.experimental.pallas import tpu as pltpu
from jax.sharding import PartitionSpec as P

UNROLL = 16
MESH = pl.DeviceIdType.MESH
CELLS = 32 * 128 * 1024
PLANES = (16, 4, 2)
WORK = (48, 32, 24)
ROWS = (64, 48, 40)
GROUP = (64, 32, 32)
OWN = (32, 16, 8)
FIRST = (16, 8, 12)
AROUND = [(ds, dy) for ds in (-1, 0, 1) for dy in (-1, 0, 1) if (ds, dy) != (0, 0)]


def lane_of(rows):
    return lax.broadcasted_iota(jnp.int32, (rows, 128), 1)


def row_of(rows):
    return lax.broadcasted_iota(jnp.int32, (rows, 128), 0)


def roll(values, shift):
    shift = shift % 128
    return values if shift == 0 else pltpu.roll(values, shift, 1)


def kernel(
    f_ref, c_ref, w_ref, g_ref, sol_ref, grad_ref, wg_ref,
    pk, tb, ef, ua, ub, fr, kk, dd, qq, tt, sv,
    c1, ua1, ub1, fr1, kk1, dd1, qq1, tt1, sv1,
    c2, ua2, ub2, fr2, kk2, dd2, qq2, sv2,
    inside0, inside1, inside2, mats,
    *rest,
):
    ex = [rest[6 * i : 6 * i + 6] for i in range(5)]
    rest = rest[30:]
    ga = [rest[2 * i : 2 * i + 2] for i in range(3)]
    po, ob, ra, rb, rc = rest[6:11]
    send_sem, recv_sem = rest[11:13]

    x, y, z = lax.axis_index("gx"), lax.axis_index("gy"), lax.axis_index("gz")
    odd = lax.rem(z, 2)

    def flip(value, parity):
        return value + parity * (3 - 2 * value)

    part = flip(x, odd)
    slab = 4 * z + part

    def peer(ds, dy):
        other = lax.rem(slab + ds + 32, 32)
        oz = lax.div(other, 4)
        ox = flip(lax.rem(other, 4), lax.rem(oz, 2))
        return (ox, lax.rem(y + dy + 4, 4), oz)

    x_peers = [(lax.rem(x + d, 4), y, z) for d in (1, 2, 3)]
    y_peers = [(x, lax.rem(y + d, 4), z) for d in (1, 2, 3)]
    z_peers = [(x, y, lax.rem(z + d, 8)) for d in range(1, 8)]
    peers = {o: peer(*o) for o in AROUND}

    barrier = pltpu.get_barrier_semaphore()
    greeted = x_peers + list(peers.values()) + [y_peers[1]] + z_peers
    for device in greeted:
        pl.semaphore_signal(barrier, inc=1, device_id=device, device_id_type=MESH)

    pending = []
    counter = [0]

    def remote(src, dst, device):
        slot = counter[0]
        counter[0] += 1
        copy = pltpu.make_async_remote_copy(
            src_ref=src, dst_ref=dst, send_sem=send_sem.at[slot], recv_sem=recv_sem.at[slot],
            device_id=device, device_id_type=MESH,
        )
        copy.start()
        pending.append(copy)
        return copy

    lane32 = lane_of(32)
    for field, ref in enumerate((c_ref, f_ref, g_ref)):
        for x1 in range(2):
            planes = [ref[4 * x1 + x0] for x0 in range(4)]
            for p in range(4):
                packed = roll(planes[0], -32 * p)
                for x0 in range(1, 4):
                    packed = jnp.where(lane32 // 32 == x0, roll(planes[x0], 32 * (x0 - p)), packed)
                pk[p, field, x1] = packed
    pl.semaphore_wait(barrier, len(greeted))
    copies = []
    for d in (1, 2, 3):
        other = lax.rem(x + d, 4)
        copies.append(remote(pk.at[flip(other, odd)], tb.at[x], (other, y, z)))

    for level, ref in enumerate((inside0, inside1, inside2)):
        rows, lanes = row_of(WORK[level]) - 8, lane_of(WORK[level]) % GROUP[level] - FIRST[level]
        own = OWN[level]
        good = (lanes >= -8) & (lanes < own + 8)
        good &= ((rows >= 0) | (y > 0)) & ((rows < own) | (y < 3))
        good &= ((lanes >= 0) | (slab > 0)) & ((lanes < own) | (slab < 31))
        ref[...] = good.astype(jnp.float32)
    src, dst = row_of(128), lane_of(128)
    for t in range(2):
        mats[t] = jnp.where(dst == (2 * (src // 64) + t) * 32 + (src % 64) // 2, 0.125, 0.0)
        mats[2 + t] = jnp.where(src == (2 * (dst // 64) + t) * 32 + (dst % 64) // 2, 1.0, 0.0)
    mats[4] = jnp.where((dst // 32 == src // 32) & (dst % 32 == 8 + (src % 32) // 2), 0.125, 0.0)
    mats[5] = jnp.where((dst // 32 == src // 32) & (src % 32 == 8 + (dst % 32) // 2), 1.0, 0.0)
    for ref in (c1, ua1, ub1, tt1, c2, ua2, ub2):
        ref[...] = jnp.zeros_like(ref)
    for ref in (tt, ua, ub, ef):
        edge = jnp.zeros(ref.shape[:-2] + (8, 128), jnp.float32)
        ref[..., 0:8, :] = edge
        ref[..., 56:64, :] = edge

    tb[x] = pk[part]
    for copy in copies:
        copy.wait_recv()

    group32 = lane32 // 64

    def build(field, unused):
        for h in range(2):
            for x1 in range(2):
                low, high = tb[h, field, x1], tb[2 + h, field, x1]
                for x0 in range(4):
                    plane = jnp.where(group32 == 0, roll(low, 16 - 32 * x0), roll(high, 80 - 32 * x0))
                    ef[field, 1 + 8 * h + 4 * x1 + x0, 16:48] = plane
        return unused

    lax.fori_loop(0, 3, build, 0)

    def pack(level, ref, bufs, count):
        zs, ys = bufs[:2]
        own, first, group = OWN[level], FIRST[level], GROUP[level]
        per = group // 8
        lanes = lane_of(own) % group
        lanes8 = lane_of(8) % group
        mine = (lanes8 >= first) & (lanes8 < first + own)

        def step(field, unused):
            for i in range(PLANES[level] // per):
                left = right = None
                for k in range(per):
                    plane = ref[field, 1 + i * per + k, 16 : 16 + own]
                    a, b = roll(plane, 8 * k - first), roll(plane, 8 * k - first - own + 8)
                    left = a if k == 0 else jnp.where(lanes // 8 == k, a, left)
                    right = b if k == 0 else jnp.where(lanes // 8 == k, b, right)
                zs[0, field, i] = left
                zs[1, field, i] = right
            for i in range(PLANES[level] // 2):
                for side, at in ((0, 16), (1, 8 + own)):
                    a, b = ref[field, 1 + 2 * i, at : at + 8], ref[field, 2 + 2 * i, at : at + 8]
                    ys[side, field, i] = jnp.where(mine, a, roll(b, group // 2))
            return unused

        lax.fori_loop(0, count, step, 0)

    def send(level, bufs):
        zs, ys, ls, rs, yl, yh = bufs
        own = OWN[level]
        low, high, face = pl.ds(0, 8), pl.ds(own + 8, 8), pl.ds(8, own)
        first, last = pl.ds(0, 8), pl.ds(own - 8, 8)
        return [
            remote(zs.at[1], ls.at[:, :, face], peers[1, 0]),
            remote(zs.at[0], rs.at[:, :, face], peers[-1, 0]),
            remote(ys.at[1], yl, peers[0, 1]),
            remote(ys.at[0], yh, peers[0, -1]),
            remote(zs.at[1, :, :, last], ls.at[:, :, low], peers[1, 1]),
            remote(zs.at[1, :, :, first], ls.at[:, :, high], peers[1, -1]),
            remote(zs.at[0, :, :, last], rs.at[:, :, low], peers[-1, 1]),
            remote(zs.at[0, :, :, first], rs.at[:, :, high], peers[-1, -1]),
        ]

    def ghosts(level, ref, count):
        planes, work, group = PLANES[level], WORK[level], GROUP[level]
        at = slice(8, 8 + work)
        lanes = lane_of(work)
        for field in range(count):
            before, after = ref[field, planes, at], ref[field, 1, at]
            ref[field, 0, at] = jnp.where(lanes < group, 0.0, roll(before, group))
            ref[field, planes + 1, at] = jnp.where(lanes >= 128 - group, 0.0, roll(after, -group))

    insides = (inside0, inside1, inside2)

    def unpack(level, ref, bufs, count):
        ls, rs, yl, yh = bufs[2:]
        own, first, group, work = OWN[level], FIRST[level], GROUP[level], WORK[level]
        per = group // 8
        lanes = lane_of(work) % group
        mine = (lanes >= first) & (lanes < first + own)
        before = lanes < first

        def step(field, unused):
            keep = insides[level][...]
            for i in range(PLANES[level] // per):
                left, right = ls[field, i], rs[field, i]
                for k in range(per):
                    plane = i * per + k
                    low, high = yl[field, plane // 2], yh[field, plane // 2]
                    if plane % 2:
                        low, high = roll(low, -(group // 2)), roll(high, -(group // 2))
                    middle = ref[field, 1 + plane, 16 : 16 + own]
                    base = jnp.concatenate([low, middle, high], axis=0)
                    sides = jnp.where(
                        before, roll(left, first - 8 - 8 * k), roll(right, first + own - 8 * k)
                    )
                    ref[field, 1 + plane, 8 : 8 + work] = jnp.where(mine, base, sides) * keep
            return unused

        lax.fori_loop(0, count, step, 0)

    def beside(ref, field, plane, work):
        here = ref[field, plane + 1, 8 : 8 + work]
        return here, [
            ref[field, plane + 2, 8 : 8 + work],
            ref[field, plane, 8 : 8 + work],
            ref[field, plane + 1, 9 : 9 + work],
            ref[field, plane + 1, 7 : 7 + work],
            roll(here, -1),
            roll(here, 1),
        ]

    def setup(level, cells, kref, dref, qref):
        work = WORK[level]
        factor = 0.5 * 0.25**level

        def step(plane, unused):
            here, around = beside(cells, 0, plane, work)
            couplings = [factor * (here + other) for other in around]
            diagonal = couplings[0]
            for coupling in couplings[1:]:
                diagonal = diagonal + coupling
            good = (insides[level][...] > 0.5) & (diagonal > 0.0)
            inverse = jnp.where(good, 1.0 / jnp.where(good, diagonal, 1.0), 0.0)
            for index, coupling in enumerate(couplings):
                kref[index, plane] = inverse * coupling
            dref[plane] = diagonal
            qref[plane] = inverse
            return unused

        lax.fori_loop(0, PLANES[level], step, 0, unroll=min(UNROLL, PLANES[level]))

    krefs, drefs, frefs, svs = (kk, kk1, kk2), (dd, dd1, dd2), (fr, fr1, fr2), (sv, sv1, sv2)

    def residual(level, ref, field, plane):
        here, around = beside(ref, field, plane, WORK[level])
        total = frefs[level][field, plane] - here
        for index in range(6):
            total = total + krefs[level][index, plane] * around[index]
        return here, total

    def sweep(level, old, new, save=None):
        weight = w_ref[level]

        def step(plane, unused):
            for field in range(2):
                here, r = residual(level, old, field, plane)
                new[field, plane + 1, 8 : 8 + WORK[level]] = here + weight * r
                if save is not None:
                    svs[level][save, field, plane] = r[8 : 8 + OWN[level]]
            return unused

        lax.fori_loop(0, PLANES[level], step, 0, unroll=min(UNROLL, PLANES[level]))
        ghosts(level, new, 2)

    def first_sweep(level, new):
        weight = w_ref[level]

        def step(plane, unused):
            for field in range(2):
                new[field, plane + 1, 8 : 8 + WORK[level]] = weight * frefs[level][field, plane]
            return unused

        lax.fori_loop(0, PLANES[level], step, 0, unroll=min(UNROLL, PLANES[level]))
        ghosts(level, new, 2)

    def defect(level, ref, out):
        work = WORK[level]

        def step(pair, unused):
            for field in range(2):
                total = None
                for side in range(2):
                    plane = 2 * pair + side
                    e = drefs[level][plane] * residual(level, ref, field, plane)[1]
                    total = e if total is None else total + e
                out[field, pair, 8 : 8 + work] = total
            return unused

        lax.fori_loop(0, PLANES[level] // 2, step, 0, unroll=min(UNROLL, PLANES[level] // 2))

    def dot(a, b):
        return jnp.dot(a, b, precision=lax.Precision.HIGHEST, preferred_element_type=jnp.float32)

    def pairs(ref, field, plane, rows):
        even = ref[field, plane, pl.ds(0, rows // 2, stride=2), :]
        return even + ref[field, plane, pl.ds(1, rows // 2, stride=2), :]

    def restricted(level, ref, field):
        if level == 0:
            a = jnp.concatenate([pairs(ref, field, m, 64) for m in range(4)], axis=0)
            b = jnp.concatenate([pairs(ref, field, 4 + m, 64) for m in range(4)], axis=0)
            return (dot(a, mats[0]) + dot(b, mats[1])).reshape(4, 32, 128)
        a = jnp.concatenate([pairs(ref, field, m, 48) for m in range(2)], axis=0)
        return dot(a, mats[4]).reshape(2, 24, 128)

    def prolong(level, ref, out):
        for field in range(2):
            if level == 0:
                w = ref[field, 1:5, 8:40].reshape(128, 128)
                for t in range(2):
                    moved = dot(w, mats[2 + t]).reshape(4, 32, 128)
                    for m in range(4):
                        out[field, 4 * t + m, pl.ds(0, 32, stride=2), :] = moved[m]
                        out[field, 4 * t + m, pl.ds(1, 32, stride=2), :] = moved[m]
            else:
                w = ref[field, 1:3, 8:32].reshape(48, 128)
                moved = dot(w, mats[5]).reshape(2, 24, 128)
                for m in range(2):
                    out[field, m, pl.ds(0, 24, stride=2), :] = moved[m]
                    out[field, m, pl.ds(1, 24, stride=2), :] = moved[m]

    def product(level, a, b, fa, fb):
        own, first = OWN[level], FIRST[level]
        lanes = lane_of(own) % GROUP[level]
        mine = (lanes >= first) & (lanes < first + own)

        def step(plane, total):
            saved = svs[level]
            value = drefs[level][plane, 8 : 8 + own] * saved[a, fa, plane] * saved[b, fb, plane]
            value = jnp.where(mine, value, 0.0)
            for tile in range(own // 8):
                total = total + value[8 * tile : 8 * tile + 8]
            return total

        return lax.fori_loop(0, PLANES[level], step, jnp.zeros((8, 128), jnp.float32))

    def gather(bufs):
        own, land = bufs
        return [
            remote(own, land.at[1 - ds, :, :, pl.ds(8 - 8 * dy, 8)], peers[ds, dy])
            for ds, dy in AROUND
        ]

    lanes2 = lane_of(24) % 32

    def gathered(land, field, plane):
        sides = jnp.where(
            lanes2 < 12, roll(land[0, field, plane], -8), roll(land[2, field, plane], 8)
        )
        mine = (lanes2 >= 12) & (lanes2 < 20)
        return jnp.where(mine, land[1, field, plane], sides) * inside2[...]

    pack(0, ef, ex[0], 3)
    copies = send(0, ex[0])

    def add_planes(pair, unused):
        tt[0, pair, 16:48] = ef[0, 1 + 2 * pair, 16:48] + ef[0, 2 + 2 * pair, 16:48]
        return unused

    lax.fori_loop(0, 8, add_planes, 0)
    early = restricted(0, tt, 0)
    for pair in range(2):
        tt1[0, pair, 8:40] = early[2 * pair] + early[2 * pair + 1]
    early = restricted(1, tt1, 0)
    own2, land2 = ga[0]
    for plane in range(2):
        own2[0, plane] = early[plane, 8:16]
        land2[1, 0, plane, 8:16] = early[plane, 8:16]
    coarse_copies = gather(ga[0])

    for copy in copies:
        copy.wait_recv()
    unpack(0, ef, ex[0], 3)
    ghosts(0, ef, 1)
    setup(0, ef, kk, dd, qq)

    def right_side(plane, unused):
        for field in range(2):
            fr[field, plane] = qq[plane] * ef[1 + field, plane + 1, 8:56]
        return unused

    lax.fori_loop(0, 16, right_side, 0)

    first_sweep(0, ua)
    sweep(0, ua, ub, 0)
    defect(0, ub, tt)

    def coarse_right_side(level, source, fine):
        for field in range(2):
            values = restricted(level, fine, field)
            for plane in range(PLANES[level + 1]):
                source(field, plane, values[plane])

    def keep1(field, plane, value):
        fr1[field, plane] = value

    coarse_right_side(0, keep1, tt)

    def add_planes_whole(pair, unused):
        tt[0, pair, 8:56] = ef[0, 1 + 2 * pair, 8:56] + ef[0, 2 + 2 * pair, 8:56]
        return unused

    lax.fori_loop(0, 8, add_planes_whole, 0)
    cells = restricted(0, tt, 0)
    for plane in range(4):
        c1[0, plane + 1, 8:40] = cells[plane] * inside1[...]
    ghosts(1, c1, 1)
    setup(1, c1, kk1, dd1, qq1)
    for copy in coarse_copies:
        copy.wait_recv()
    for plane in range(2):
        c2[0, plane + 1, 8:32] = gathered(land2, 0, plane)
    ghosts(2, c2, 1)
    setup(2, c2, kk2, dd2, qq2)

    def scale1():
        for field in range(2):
            for plane in range(4):
                fr1[field, plane] = qq1[plane] * fr1[field, plane]

    def middle(cycle):
        first_sweep(1, ua1)
        sweep(1, ua1, ub1, 2 * cycle)
        defect(1, ub1, tt1)
        own, land = ga[1 + cycle]

        def keep2(field, plane, value):
            scaled = qq2[plane, 8:16] * value[8:16]
            own[field, plane] = scaled
            land[1, field, plane, 8:16] = scaled

        coarse_right_side(1, keep2, tt1)
        copies = gather(ga[1 + cycle])
        if cycle == 0:
            pack(1, ub1, ex[1], 2)
            more = send(1, ex[1])
        for copy in copies:
            copy.wait_recv()
        for field in range(2):
            for plane in range(2):
                fr2[field, plane] = gathered(land, field, plane)
        first_sweep(2, ua2)
        refs = (ua2, ub2)
        for index in range(1, 8):
            save = cycle if index == 3 + cycle else None
            sweep(2, refs[(index + 1) % 2], refs[index % 2], save)
        prolong(1, ub2, tt1)
        if cycle == 0:
            for copy in more:
                copy.wait_recv()
            unpack(1, ub1, ex[1], 2)
        for field in range(2):
            for plane in range(4):
                ub1[field, plane + 1, 8:40] = (
                    ub1[field, plane + 1, 8:40] + tt1[field, plane // 2, 8:40]
                )
        ghosts(1, ub1, 2)
        sweep(1, ub1, ua1, 1 + 2 * cycle)
        sweep(1, ua1, ub1)

    def correct(ref):
        prolong(0, ub1, tt)

        def step(plane, unused):
            for field in range(2):
                ref[field, plane + 1, 16:48] = (
                    ref[field, plane + 1, 16:48] + tt[field, lax.div(plane, 2), 16:48]
                )
            return unused

        lax.fori_loop(0, 16, step, 0)

    def fine_halo(ref, bufs):
        pack(0, ref, bufs, 2)
        for copy in send(0, bufs):
            copy.wait_recv()
        unpack(0, ref, bufs, 2)
        ghosts(0, ref, 2)

    scale1()
    middle(0)
    correct(ub)
    fine_halo(ub, ex[2])
    sweep(0, ub, ua)
    sweep(0, ua, ub, 1)
    sweep(0, ub, ua, 2)
    sweep(0, ua, ub)
    defect(0, ub, tt)

    def keep_c1(field, plane, value):
        ua1[field, plane + 1, 8:40] = value

    coarse_right_side(0, keep_c1, tt)
    pack(1, ua1, ex[3], 2)
    for copy in send(1, ex[3]):
        copy.wait_recv()
    unpack(1, ua1, ex[3], 2)
    for field in range(2):
        for plane in range(4):
            fr1[field, plane] = qq1[plane] * ua1[field, plane + 1, 8:40]
    middle(1)
    correct(ub)
    fine_halo(ub, ex[4])
    sweep(0, ub, ua, 3)

    scale = 1.0 / CELLS
    sums = [
        2.0 * (product(0, 0, 3, 0, 1) + product(0, 3, 0, 0, 1)) + 4.0 * product(0, 1, 2, 0, 1),
        16.0
        * (
            product(1, 0, 3, 0, 1)
            + product(1, 3, 0, 0, 1)
            + product(1, 1, 2, 0, 1)
            + product(1, 2, 1, 0, 1)
        ),
        512.0 * (product(2, 0, 1, 0, 1) + product(2, 1, 0, 0, 1)),
    ]
    for level in range(3):
        ra[z, 8 * level : 8 * level + 8] = sums[level] * scale
    copies_a = [remote(ra.at[z], ra.at[z], device) for device in z_peers]

    sweep(0, ua, ub)

    def leave(field, unused):
        for h in range(2):
            for x1 in range(2):
                planes = [ub[field, 1 + 8 * h + 4 * x1 + x0, 16:48] for x0 in range(4)]
                for g in range(2):
                    packed = roll(planes[0], -64 * g - 16)
                    for x0 in range(1, 4):
                        packed = jnp.where(
                            lane32 // 32 == x0, roll(planes[x0], 32 * x0 - 64 * g - 16), packed
                        )
                    po[2 * g + h, field, x1] = packed
        return unused

    lax.fori_loop(0, 2, leave, 0)
    copies_o = []
    for d in (1, 2, 3):
        other = lax.rem(x + d, 4)
        copies_o.append(remote(po.at[other], ob.at[part], (other, y, z)))
    ob[part] = po[x]

    for copy in copies_a:
        copy.wait_recv()
    total = ra[0]
    for index in range(1, 8):
        total = total + ra[index]
    rb[y] = total
    copies_b = [remote(rb.at[y], rb.at[y], device) for device in y_peers]

    for copy in copies_o:
        copy.wait_recv()
    for field, ref in enumerate((sol_ref, grad_ref)):
        for x1 in range(2):
            quarters = [ob[p, field, x1] for p in range(4)]
            for x0 in range(4):
                out = roll(quarters[0], -32 * x0)
                for p in range(1, 4):
                    out = jnp.where(lane32 // 32 == p, roll(quarters[p], 32 * (p - x0)), out)
                ref[4 * x1 + x0] = out

    for copy in copies_b:
        copy.wait_recv()
    total = rb[0]
    for index in range(1, 4):
        total = total + rb[index]
    rc[x] = total
    copies_c = [remote(rc.at[x], rc.at[x], device) for device in x_peers]
    for copy in copies_c:
        copy.wait_recv()
    total = rc[0]
    for index in range(1, 4):
        total = total + rc[index]
    for level in range(3):
        wg_ref[level] = jnp.sum(total[8 * level : 8 * level + 8])
    for copy in pending:
        copy.wait_send()


def f32(*shape):
    return pltpu.VMEM(shape, jnp.float32)


def exchange_buffers(level, count):
    own, strips, half = OWN[level], PLANES[level] * 8 // GROUP[level], PLANES[level] // 2
    return [
        f32(2, count, strips, own, 128),
        f32(2, count, half, 8, 128),
        f32(count, strips, own + 16, 128),
        f32(count, strips, own + 16, 128),
        f32(count, half, 8, 128),
        f32(count, half, 8, 128),
    ]


def level_buffers(level):
    planes, work, rows, own = PLANES[level], WORK[level], ROWS[level], OWN[level]
    out = [
        f32(2, planes + 2, rows, 128),
        f32(2, planes + 2, rows, 128),
        f32(2, planes, work, 128),
        f32(6, planes, work, 128),
        f32(planes, work, 128),
        f32(planes, work, 128),
    ]
    if level < 2:
        out.append(f32(2, planes // 2, rows, 128))
    out.append(f32(4 if level < 2 else 2, 2, planes, own, 128))
    return out


def body(source_term, conductivity, jacobi_weights, cotangent):
    scratch = [f32(4, 3, 2, 32, 128), f32(4, 3, 2, 32, 128), f32(3, 18, 64, 128)]
    scratch += level_buffers(0)
    scratch += [f32(1, 6, 48, 128)] + level_buffers(1)
    scratch += [f32(1, 4, 40, 128)] + level_buffers(2)
    scratch += [f32(WORK[level], 128) for level in range(3)] + [f32(6, 128, 128)]
    for level, count in ((0, 3), (1, 2), (0, 2), (1, 2), (0, 2)):
        scratch += exchange_buffers(level, count)
    for count in (1, 2, 2):
        scratch += [f32(count, 2, 8, 128), f32(3, count, 2, 24, 128)]
    scratch += [f32(4, 2, 2, 32, 128), f32(4, 2, 2, 32, 128)]
    scratch += [f32(8, 24, 128), f32(4, 24, 128), f32(4, 24, 128)]
    copies = 3 + 8 * 8 + 3 + 13
    scratch += [pltpu.SemaphoreType.DMA((copies,)), pltpu.SemaphoreType.DMA((copies,))]
    vmem = pl.BlockSpec(memory_space=pltpu.VMEM)
    smem = pl.BlockSpec(memory_space=pltpu.SMEM)
    block = jax.ShapeDtypeStruct(source_term.shape, jnp.float32)
    return pl.pallas_call(
        kernel,
        out_shape=(block, block, jax.ShapeDtypeStruct((3,), jnp.float32)),
        in_specs=[vmem, vmem, smem, vmem],
        out_specs=(vmem, vmem, smem),
        scratch_shapes=scratch,
        compiler_params=pltpu.CompilerParams(
            collective_id=0, has_side_effects=True, vmem_limit_bytes=48 * 2**20
        ),
    )(source_term, conductivity, jacobi_weights, cotangent)


def solution(mesh):
    return jax.shard_map(
        body,
        mesh=mesh,
        in_specs=(P("gx", "gy", "gz"), P("gx", "gy", "gz"), P(), P("gx", "gy", "gz")),
        out_specs=(P("gx", "gy", "gz"), P("gx", "gy", "gz"), P()),
        check_vma=False,
    )
```

```python
import functools

import jax
import jax.numpy as jnp
from jax import lax
from jax.experimental import pallas as pl
from jax.experimental.pallas import tpu as pltpu
from jax.sharding import PartitionSpec as P

MESH = pl.DeviceIdType.MESH
CELLS = 32 * 128 * 1024
PLANES = (16, 4, 2)
WORK = (48, 32, 24)
ROWS = (64, 48, 40)
GROUP = (64, 32, 32)
OWN = (32, 16, 8)
FIRST = (16, 8, 12)
AROUND = [(ds, dy) for ds in (-1, 0, 1) for dy in (-1, 0, 1) if (ds, dy) != (0, 0)]


def lane_of(rows):
    return lax.broadcasted_iota(jnp.int32, (rows, 128), 1)


def row_of(rows):
    return lax.broadcasted_iota(jnp.int32, (rows, 128), 0)


def roll(values, shift):
    shift = shift % 128
    return values if shift == 0 else pltpu.roll(values, shift, 1)


def kernel(
    f_hbm, c_hbm, w_hbm, g_hbm, sol_ref, grad_ref, wg_ref,
    f_ref, c_ref, g_ref, w_ref, load_sem, pkc, pkf, tbc, tbf, ef, ua, ub, fr, kk, dd, qq, tt, sv,
    c1, ua1, ub1, fr1, kk1, dd1, qq1, tt1, sv1,
    c2, ua2, ub2, fr2, kk2, dd2, qq2, sv2,
    inside0, inside1, inside2, mats,
    *rest,
):
    ex = [rest[6 * i : 6 * i + 6] for i in range(5)]
    rest = rest[30:]
    ga = [rest[2 * i : 2 * i + 2] for i in range(3)]
    po, ob, ra, rb, rc = rest[6:11]
    send_sem, recv_sem = rest[11:13]

    x, y, z = lax.axis_index("gx"), lax.axis_index("gy"), lax.axis_index("gz")
    odd = lax.rem(z, 2)

    def flip(value, parity):
        return value + parity * (3 - 2 * value)

    part = flip(x, odd)
    slab = 4 * z + part

    def peer(ds, dy):
        other = lax.rem(slab + ds + 32, 32)
        oz = lax.div(other, 4)
        ox = flip(lax.rem(other, 4), lax.rem(oz, 2))
        return (ox, lax.rem(y + dy + 4, 4), oz)

    x_peers = [(lax.rem(x + d, 4), y, z) for d in (1, 2, 3)]
    y_peers = [(x, lax.rem(y + d, 4), z) for d in (1, 2, 3)]
    z_peers = [(x, y, lax.rem(z + d, 8)) for d in range(1, 8)]
    peers = {o: peer(*o) for o in AROUND}

    loads = [
        pltpu.make_async_copy(src, dst, load_sem.at[index])
        for index, (src, dst) in enumerate(
            ((c_hbm, c_ref), (f_hbm, f_ref), (g_hbm, g_ref), (w_hbm, w_ref))
        )
    ]
    for load in loads:
        load.start()
    barrier = pltpu.get_barrier_semaphore()
    greeted = x_peers + list(peers.values()) + [y_peers[1]] + z_peers
    for device in greeted:
        pl.semaphore_signal(barrier, inc=1, device_id=device, device_id_type=MESH)

    pending = []
    counter = [0]

    def remote(src, dst, device):
        slot = counter[0]
        counter[0] += 1
        copy = pltpu.make_async_remote_copy(
            src_ref=src, dst_ref=dst, send_sem=send_sem.at[slot], recv_sem=recv_sem.at[slot],
            device_id=device, device_id_type=MESH,
        )
        copy.start()
        pending.append(copy)
        return copy

    lane32 = lane_of(32)

    def quarters(ref, out, field):
        for x1 in range(2):
            planes = [ref[4 * x1 + x0] for x0 in range(4)]
            for p in range(4):
                packed = roll(planes[0], -32 * p)
                for x0 in range(1, 4):
                    packed = jnp.where(lane32 // 32 == x0, roll(planes[x0], 32 * (x0 - p)), packed)
                out[p, field, x1] = packed

    def scatter(out, land):
        copies = []
        for d in (1, 2, 3):
            other = lax.rem(x + d, 4)
            copies.append(remote(out.at[flip(other, odd)], land.at[x], (other, y, z)))
        return copies

    loads[0].wait()
    quarters(c_ref, pkc, 0)
    pl.semaphore_wait(barrier, len(greeted))
    copies_c = scatter(pkc, tbc)
    loads[1].wait()
    quarters(f_ref, pkf, 0)
    loads[2].wait()
    quarters(g_ref, pkf, 1)
    copies_f = scatter(pkf, tbf)
    loads[3].wait()

    for level, ref in enumerate((inside0, inside1, inside2)):
        rows, lanes = row_of(WORK[level]) - 8, lane_of(WORK[level]) % GROUP[level] - FIRST[level]
        own = OWN[level]
        good = (lanes >= -8) & (lanes < own + 8)
        good &= ((rows >= 0) | (y > 0)) & ((rows < own) | (y < 3))
        good &= ((lanes >= 0) | (slab > 0)) & ((lanes < own) | (slab < 31))
        ref[...] = good.astype(jnp.float32)
    src, dst = row_of(128), lane_of(128)
    for t in range(2):
        mats[t] = jnp.where(dst == (2 * (src // 64) + t) * 32 + (src % 64) // 2, 0.125, 0.0)
        mats[2 + t] = jnp.where(src == (2 * (dst // 64) + t) * 32 + (dst % 64) // 2, 1.0, 0.0)
    mats[4] = jnp.where((dst // 32 == src // 32) & (dst % 32 == 8 + (src % 32) // 2), 0.125, 0.0)
    mats[5] = jnp.where((dst // 32 == src // 32) & (src % 32 == 8 + (dst % 32) // 2), 1.0, 0.0)
    for ref in (c1, ua1, ub1, tt1, c2, ua2, ub2):
        ref[...] = jnp.zeros_like(ref)
    for ref in (tt, ua, ub, ef):
        edge = jnp.zeros(ref.shape[:-2] + (8, 128), jnp.float32)
        ref[..., 0:8, :] = edge
        ref[..., 56:64, :] = edge

    group32 = lane32 // 64

    def build(land, field, to):
        for h in range(2):
            for x1 in range(2):
                low, high = land[h, field, x1], land[2 + h, field, x1]
                for x0 in range(4):
                    plane = jnp.where(group32 == 0, roll(low, 16 - 32 * x0), roll(high, 80 - 32 * x0))
                    ef[to, 1 + 8 * h + 4 * x1 + x0, 16:48] = plane

    def pack(level, ref, bufs, count, nine=False, start=0):
        zs, ys = bufs[:2]
        own, first, group = OWN[level], FIRST[level], GROUP[level]
        per = group // 8
        lanes = lane_of(own) % group
        lanes8 = lane_of(8) % group
        mine = (lanes8 >= first) & (lanes8 < first + own)

        def step(field, unused):
            at = start + field
            ninths = []
            for i in range(PLANES[level] // per):
                left = right = left9 = right9 = None
                for k in range(per):
                    plane = ref[at, 1 + i * per + k, 16 : 16 + own]
                    a, b = roll(plane, 8 * k - first), roll(plane, 8 * k - first - own + 8)
                    left = a if k == 0 else jnp.where(lanes // 8 == k, a, left)
                    right = b if k == 0 else jnp.where(lanes // 8 == k, b, right)
                    if nine:
                        left9 = a if k == 0 else jnp.where(lanes // 8 == (k + 1) % per, a, left9)
                        right9 = b if k == 0 else jnp.where(lanes // 8 == (k - 1) % per, b, right9)
                zs[0, field, i] = left
                zs[1, field, i] = right
                ninths.append((left9, right9))
            if nine:
                zs[0, field, 2] = jnp.where(lanes % 8 < 4, ninths[0][0], roll(ninths[1][0], 4))
                zs[1, field, 2] = jnp.where(lanes % 8 >= 4, ninths[0][1], roll(ninths[1][1], -4))
            for i in range(PLANES[level] // 2):
                for side, row in ((0, 16), (1, 8 + own)):
                    a, b = ref[at, 1 + 2 * i, row : row + 8], ref[at, 2 + 2 * i, row : row + 8]
                    ys[side, field, i] = jnp.where(mine, a, roll(b, group // 2))
                if nine:
                    for side, row in ((0, 24), (1, 39)):
                        a, b = ref[at, 1 + 2 * i, row : row + 1], ref[at, 2 + 2 * i, row : row + 1]
                        ys[side, field, 8, i : i + 1] = jnp.where(mine[:1], a, roll(b, group // 2))
            return unused

        lax.fori_loop(0, count, step, 0)

    def send(level, bufs):
        zs, ys, ls, rs, yl, yh = bufs
        own = OWN[level]
        low, high, face = pl.ds(0, 8), pl.ds(own + 8, 8), pl.ds(8, own)
        first, last = pl.ds(0, 8), pl.ds(own - 8, 8)
        strips = pl.ds(0, PLANES[level] * 8 // GROUP[level])
        return [
            remote(zs.at[1], ls.at[:, :, face], peers[1, 0]),
            remote(zs.at[0], rs.at[:, :, face], peers[-1, 0]),
            remote(ys.at[1], yl, peers[0, 1]),
            remote(ys.at[0], yh, peers[0, -1]),
            remote(zs.at[1, :, strips, last], ls.at[:, strips, low], peers[1, 1]),
            remote(zs.at[1, :, strips, first], ls.at[:, strips, high], peers[1, -1]),
            remote(zs.at[0, :, strips, last], rs.at[:, strips, low], peers[-1, 1]),
            remote(zs.at[0, :, strips, first], rs.at[:, strips, high], peers[-1, -1]),
        ]

    def ghosts(level, ref, count):
        planes, work, group = PLANES[level], WORK[level], GROUP[level]
        at = slice(8, 8 + work)
        lanes = lane_of(work)
        for field in range(count):
            before, after = ref[field, planes, at], ref[field, 1, at]
            ref[field, 0, at] = jnp.where(lanes < group, 0.0, roll(before, group))
            ref[field, planes + 1, at] = jnp.where(lanes >= 128 - group, 0.0, roll(after, -group))

    insides = (inside0, inside1, inside2)
    has_left, has_right = (slab > 0).astype(jnp.float32), (slab < 31).astype(jnp.float32)
    has_low, has_high = (y > 0).astype(jnp.float32), (y < 3).astype(jnp.float32)

    def unpack(level, ref, bufs, count, nine=False, start=0):
        ls, rs, yl, yh = bufs[2:]
        own, first, group, work = OWN[level], FIRST[level], GROUP[level], WORK[level]
        per = group // 8
        lanes = lane_of(work) % group
        mine = (lanes >= first) & (lanes < first + own)
        before = lanes < first
        lanes9 = lane_of(own) % group

        def step(field, unused):
            at = start + field
            keep = insides[level][...]
            for i in range(PLANES[level] // per):
                left, right = ls[field, i], rs[field, i]
                for k in range(per):
                    plane = i * per + k
                    low, high = yl[field, plane // 2], yh[field, plane // 2]
                    if plane % 2:
                        low, high = roll(low, -(group // 2)), roll(high, -(group // 2))
                    middle = ref[at, 1 + plane, 16 : 16 + own]
                    base = jnp.concatenate([low, middle, high], axis=0)
                    sides = jnp.where(
                        before, roll(left, first - 8 - 8 * k), roll(right, first + own - 8 * k)
                    )
                    ref[at, 1 + plane, 8 : 8 + work] = jnp.where(mine, base, sides) * keep
                    if nine:
                        left9 = roll(ls[field, 2, 8 : 8 + own], 8 + 4 * i - 8 * k) * has_left
                        right9 = roll(rs[field, 2, 8 : 8 + own], 48 - 4 * i - 8 * k) * has_right
                        middle = ref[at, 1 + plane, 16 : 16 + own]
                        middle = jnp.where(lanes9 == 7, left9, middle)
                        middle = jnp.where(lanes9 == 56, right9, middle)
                        ref[at, 1 + plane, 16 : 16 + own] = middle
                        for rows, row, has in ((yl, 7, has_low), (yh, 56, has_high)):
                            ninth = rows[field, 8, plane // 2 : plane // 2 + 1]
                            if plane % 2:
                                ninth = roll(ninth, -(group // 2))
                            ref[at, 1 + plane, row : row + 1] = jnp.where(mine[:1], ninth * has, 0.0)
            return unused

        lax.fori_loop(0, count, step, 0)

    def beside(ref, field, plane, work):
        here = ref[field, plane + 1, 8 : 8 + work]
        return here, [
            ref[field, plane + 2, 8 : 8 + work],
            ref[field, plane, 8 : 8 + work],
            ref[field, plane + 1, 9 : 9 + work],
            ref[field, plane + 1, 7 : 7 + work],
            roll(here, -1),
            roll(here, 1),
        ]

    def setup(level, cells, kref, dref, qref):
        work = WORK[level]
        factor = 0.5 * 0.25**level

        def step(plane, unused):
            here, around = beside(cells, 0, plane, work)
            couplings = [factor * (here + other) for other in around]
            diagonal = couplings[0]
            for coupling in couplings[1:]:
                diagonal = diagonal + coupling
            good = (insides[level][...] > 0.5) & (diagonal > 0.0)
            inverse = jnp.where(good, 1.0 / jnp.where(good, diagonal, 1.0), 0.0)
            for index, coupling in enumerate(couplings):
                kref[index, plane] = inverse * coupling
            dref[plane] = diagonal
            qref[plane] = inverse
            return unused

        lax.fori_loop(0, PLANES[level], step, 0, unroll=True)

    krefs, drefs, frefs, svs = (kk, kk1, kk2), (dd, dd1, dd2), (fr, fr1, fr2), (sv, sv1, sv2)

    def residual(level, ref, field, plane):
        here, around = beside(ref, field, plane, WORK[level])
        total = frefs[level][field, plane] - here
        for index in range(6):
            total = total + krefs[level][index, plane] * around[index]
        return here, total

    def sweep(level, old, new, save=None):
        weight = w_ref[level]

        def step(plane, unused):
            for field in range(2):
                here, r = residual(level, old, field, plane)
                new[field, plane + 1, 8 : 8 + WORK[level]] = here + weight * r
                if save is not None:
                    svs[level][save, field, plane] = r[8 : 8 + OWN[level]]
            return unused

        lax.fori_loop(0, PLANES[level], step, 0, unroll=True)
        ghosts(level, new, 2)

    def first_sweep(level, new):
        weight = w_ref[level]

        def step(plane, unused):
            for field in range(2):
                new[field, plane + 1, 8 : 8 + WORK[level]] = weight * frefs[level][field, plane]
            return unused

        lax.fori_loop(0, PLANES[level], step, 0, unroll=True)
        ghosts(level, new, 2)

    def defect(level, ref, out, save=None):
        work = WORK[level]

        def step(pair, unused):
            for field in range(2):
                total = None
                for side in range(2):
                    plane = 2 * pair + side
                    r = residual(level, ref, field, plane)[1]
                    if save is not None:
                        svs[level][save, field, plane] = r[8 : 8 + OWN[level]]
                    e = drefs[level][plane] * r
                    total = e if total is None else total + e
                out[field, pair, 8 : 8 + work] = total
            return unused

        lax.fori_loop(0, PLANES[level] // 2, step, 0, unroll=True)

    def dot(a, b):
        return jnp.dot(a, b, precision=lax.Precision.HIGHEST, preferred_element_type=jnp.float32)

    def pairs(ref, field, plane, rows):
        even = ref[field, plane, pl.ds(0, rows // 2, stride=2), :]
        return even + ref[field, plane, pl.ds(1, rows // 2, stride=2), :]

    def restricted(level, ref, field):
        if level == 0:
            a = jnp.concatenate([pairs(ref, field, m, 64) for m in range(4)], axis=0)
            b = jnp.concatenate([pairs(ref, field, 4 + m, 64) for m in range(4)], axis=0)
            return (dot(a, mats[0]) + dot(b, mats[1])).reshape(4, 32, 128)
        a = jnp.concatenate([pairs(ref, field, m, 48) for m in range(2)], axis=0)
        return dot(a, mats[4]).reshape(2, 24, 128)

    def prolong(level, ref, out):
        for field in range(2):
            if level == 0:
                w = ref[field, 1:5, 8:40].reshape(128, 128)
                for t in range(2):
                    moved = dot(w, mats[2 + t]).reshape(4, 32, 128)
                    for m in range(4):
                        out[field, 4 * t + m, pl.ds(0, 32, stride=2), :] = moved[m]
                        out[field, 4 * t + m, pl.ds(1, 32, stride=2), :] = moved[m]
            else:
                w = ref[field, 1:3, 8:32].reshape(48, 128)
                moved = dot(w, mats[5]).reshape(2, 24, 128)
                for m in range(2):
                    out[field, m, pl.ds(0, 24, stride=2), :] = moved[m]
                    out[field, m, pl.ds(1, 24, stride=2), :] = moved[m]

    def product(level, a, b, fa, fb):
        own, first = OWN[level], FIRST[level]
        lanes = lane_of(own) % GROUP[level]
        mine = (lanes >= first) & (lanes < first + own)

        def step(plane, total):
            saved = svs[level]
            value = drefs[level][plane, 8 : 8 + own] * saved[a, fa, plane] * saved[b, fb, plane]
            value = jnp.where(mine, value, 0.0)
            for tile in range(own // 8):
                total = total + value[8 * tile : 8 * tile + 8]
            return total

        return lax.fori_loop(0, PLANES[level], step, jnp.zeros((8, 128), jnp.float32))

    def gather(bufs):
        own, land = bufs
        return [
            remote(own, land.at[1 - ds, :, :, pl.ds(8 - 8 * dy, 8)], peers[ds, dy])
            for ds, dy in AROUND
        ]

    lanes2 = lane_of(24) % 32

    def gathered(land, field, plane):
        sides = jnp.where(
            lanes2 < 12, roll(land[0, field, plane], -8), roll(land[2, field, plane], 8)
        )
        mine = (lanes2 >= 12) & (lanes2 < 20)
        return jnp.where(mine, land[1, field, plane], sides) * inside2[...]

    tbc[x] = pkc[part]
    for copy in copies_c:
        copy.wait_recv()
    build(tbc, 0, 0)
    pack(0, ef, ex[0], 1, True)
    copies_c = send(0, ex[0])
    tbf[x] = pkf[part]
    for copy in copies_f:
        copy.wait_recv()
    for field in range(2):
        build(tbf, field, 1 + field)
    pack(0, ef, ex[1], 2, start=1)
    copies_f = send(0, ex[1])

    def add_planes(pair, unused):
        tt[0, pair, 16:48] = ef[0, 1 + 2 * pair, 16:48] + ef[0, 2 + 2 * pair, 16:48]
        return unused

    lax.fori_loop(0, 8, add_planes, 0)
    early = restricted(0, tt, 0)
    for pair in range(2):
        tt1[0, pair, 8:40] = early[2 * pair] + early[2 * pair + 1]
    early = restricted(1, tt1, 0)
    own2, land2 = ga[0]
    for plane in range(2):
        own2[0, plane] = early[plane, 8:16]
        land2[1, 0, plane, 8:16] = early[plane, 8:16]
    coarse_copies = gather(ga[0])

    for copy in copies_c:
        copy.wait_recv()
    unpack(0, ef, ex[0], 1, True)
    ghosts(0, ef, 1)
    setup(0, ef, kk, dd, qq)

    def add_planes_whole(pair, unused):
        tt[0, pair, 8:56] = ef[0, 1 + 2 * pair, 8:56] + ef[0, 2 + 2 * pair, 8:56]
        return unused

    lax.fori_loop(0, 8, add_planes_whole, 0)
    cells = restricted(0, tt, 0)
    for plane in range(4):
        c1[0, plane + 1, 8:40] = cells[plane] * inside1[...]
    ghosts(1, c1, 1)
    setup(1, c1, kk1, dd1, qq1)
    for copy in coarse_copies:
        copy.wait_recv()
    for plane in range(2):
        c2[0, plane + 1, 8:32] = gathered(land2, 0, plane)
    ghosts(2, c2, 1)
    setup(2, c2, kk2, dd2, qq2)

    for copy in copies_f:
        copy.wait_recv()
    unpack(0, ef, ex[1], 2, start=1)

    def right_side(plane, unused):
        for field in range(2):
            fr[field, plane] = qq[plane] * ef[1 + field, plane + 1, 8:56]
        return unused

    lax.fori_loop(0, 16, right_side, 0)

    first_sweep(0, ua)
    sweep(0, ua, ub, 0)
    defect(0, ub, tt, 3)

    def coarse_right_side(level, source, fine):
        for field in range(2):
            values = restricted(level, fine, field)
            for plane in range(PLANES[level + 1]):
                source(field, plane, values[plane])

    def keep1(field, plane, value):
        fr1[field, plane] = value

    coarse_right_side(0, keep1, tt)

    def scale1():
        for field in range(2):
            for plane in range(4):
                fr1[field, plane] = qq1[plane] * fr1[field, plane]

    def middle(cycle):
        first_sweep(1, ua1)
        sweep(1, ua1, ub1, 2 * cycle)
        defect(1, ub1, tt1)
        own, land = ga[1 + cycle]

        def keep2(field, plane, value):
            scaled = qq2[plane, 8:16] * value[8:16]
            own[field, plane] = scaled
            land[1, field, plane, 8:16] = scaled

        coarse_right_side(1, keep2, tt1)
        copies = gather(ga[1 + cycle])
        if cycle == 1:
            pack(1, ub1, ex[2], 2)
            more = send(1, ex[2])
        for copy in copies:
            copy.wait_recv()
        for field in range(2):
            for plane in range(2):
                fr2[field, plane] = gathered(land, field, plane)
        first_sweep(2, ua2)
        refs = (ua2, ub2)
        for index in range(1, 8):
            save = cycle if index == 3 + cycle else None
            sweep(2, refs[(index + 1) % 2], refs[index % 2], save)
        prolong(1, ub2, tt1)
        if cycle == 1:
            for copy in more:
                copy.wait_recv()
            unpack(1, ub1, ex[2], 2)
        for field in range(2):
            for plane in range(4):
                ub1[field, plane + 1, 8:40] = (
                    ub1[field, plane + 1, 8:40] + tt1[field, plane // 2, 8:40]
                )
        ghosts(1, ub1, 2)
        sweep(1, ub1, ua1, 1 + 2 * cycle)
        sweep(1, ua1, ub1)

    def correct(ref):
        prolong(0, ub1, tt)

        def step(plane, unused):
            for field in range(2):
                ref[field, plane + 1, 16:48] = (
                    ref[field, plane + 1, 16:48] + tt[field, lax.div(plane, 2), 16:48]
                )
            return unused

        lax.fori_loop(0, 16, step, 0, unroll=4)

    scale1()
    middle(0)
    correct(ub)
    pack(0, ub, ex[3], 2, True)
    for copy in send(0, ex[3]):
        copy.wait_recv()
    unpack(0, ub, ex[3], 2, True)
    ghosts(0, ub, 2)
    sweep(0, ub, ua)
    sweep(0, ua, ub, 1)
    sweep(0, ub, ua, 2)
    sweep(0, ua, ub)
    defect(0, ub, tt, 4)
    coarse_right_side(0, keep1, tt)
    scale1()
    middle(1)
    correct(ub)
    pack(0, ub, ex[4], 2)
    copies = send(0, ex[4])

    own_lanes = (lane32 % 64 >= 16) & (lane32 % 64 < 48)

    def corrected(plane, total):
        value = None
        for field in range(2):
            change = sv[0, 1 - field, plane] - sv[3, 1 - field, plane]
            term = change * tt[field, lax.div(plane, 2), 16:48]
            value = term if value is None else value + term
        value = jnp.where(own_lanes, value * dd[plane, 8:40], 0.0)
        return total + ((value[0:8] + value[8:16]) + (value[16:24] + value[24:32]))

    moved = lax.fori_loop(0, 16, corrected, jnp.zeros((8, 128), jnp.float32), unroll=4)
    scale = 1.0 / CELLS
    sums = [
        2.0 * (product(0, 0, 4, 0, 1) + product(0, 4, 0, 0, 1) - moved * (1.0 / w_ref[0]))
        + 4.0 * product(0, 1, 2, 0, 1),
        16.0
        * (
            product(1, 0, 3, 0, 1)
            + product(1, 3, 0, 0, 1)
            + product(1, 1, 2, 0, 1)
            + product(1, 2, 1, 0, 1)
        ),
        512.0 * (product(2, 0, 1, 0, 1) + product(2, 1, 0, 0, 1)),
    ]
    for level in range(3):
        ra[z, 8 * level : 8 * level + 8] = sums[level] * scale
    copies_a = [remote(ra.at[z], ra.at[z], device) for device in z_peers]

    for copy in copies:
        copy.wait_recv()
    unpack(0, ub, ex[4], 2)
    ghosts(0, ub, 2)
    sweep(0, ub, ua)
    for copy in copies_a:
        copy.wait_recv()
    total = ra[0]
    for index in range(1, 8):
        total = total + ra[index]
    rb[y] = total
    copies_b = [remote(rb.at[y], rb.at[y], device) for device in y_peers]
    sweep(0, ua, ub)

    def leave(field, unused):
        for h in range(2):
            for x1 in range(2):
                planes = [ub[field, 1 + 8 * h + 4 * x1 + x0, 16:48] for x0 in range(4)]
                for g in range(2):
                    packed = roll(planes[0], -64 * g - 16)
                    for x0 in range(1, 4):
                        packed = jnp.where(
                            lane32 // 32 == x0, roll(planes[x0], 32 * x0 - 64 * g - 16), packed
                        )
                    po[2 * g + h, field, x1] = packed
        return unused

    lax.fori_loop(0, 2, leave, 0)
    copies_o = []
    for d in (1, 2, 3):
        other = lax.rem(x + d, 4)
        copies_o.append(remote(po.at[other], ob.at[part], (other, y, z)))
    ob[part] = po[x]

    for copy in copies_b:
        copy.wait_recv()
    total = rb[0]
    for index in range(1, 4):
        total = total + rb[index]
    rc[x] = total
    copies_c = [remote(rc.at[x], rc.at[x], device) for device in x_peers]

    for copy in copies_o:
        copy.wait_recv()
    for field, ref in enumerate((sol_ref, grad_ref)):
        for x1 in range(2):
            parts = [ob[p, field, x1] for p in range(4)]
            for x0 in range(4):
                out = roll(parts[0], -32 * x0)
                for p in range(1, 4):
                    out = jnp.where(lane32 // 32 == p, roll(parts[p], 32 * (p - x0)), out)
                ref[4 * x1 + x0] = out

    for copy in copies_c:
        copy.wait_recv()
    total = rc[0]
    for index in range(1, 4):
        total = total + rc[index]
    for level in range(3):
        wg_ref[level] = jnp.sum(total[8 * level : 8 * level + 8])
    for copy in pending:
        copy.wait_send()


def f32(*shape):
    return pltpu.VMEM(shape, jnp.float32)


def exchange_buffers(level, count, nine):
    own, strips, half = OWN[level], PLANES[level] * 8 // GROUP[level] + nine, PLANES[level] // 2 + nine
    return [
        f32(2, count, strips, own, 128),
        f32(2, count, half, 8, 128),
        f32(count, strips, own + 16, 128),
        f32(count, strips, own + 16, 128),
        f32(count, half, 8, 128),
        f32(count, half, 8, 128),
    ]


def level_buffers(level):
    planes, work, rows, own = PLANES[level], WORK[level], ROWS[level], OWN[level]
    out = [
        f32(2, planes + 2, rows, 128),
        f32(2, planes + 2, rows, 128),
        f32(2, planes, work, 128),
        f32(6, planes, work, 128),
        f32(planes, work, 128),
        f32(planes, work, 128),
    ]
    if level < 2:
        out.append(f32(2, planes // 2, rows, 128))
    out.append(f32((5, 4, 2)[level], 2, planes, own, 128))
    return out


def body(source_term, conductivity, jacobi_weights, cotangent):
    block = source_term.shape
    scratch = [f32(*block), f32(*block), f32(*block), pltpu.SMEM((3,), jnp.float32)]
    scratch += [pltpu.SemaphoreType.DMA((4,))]
    scratch += [f32(4, count, 2, 32, 128) for count in (1, 2, 1, 2)] + [f32(3, 18, 64, 128)]
    scratch += level_buffers(0)
    scratch += [f32(1, 6, 48, 128)] + level_buffers(1)
    scratch += [f32(1, 4, 40, 128)] + level_buffers(2)
    scratch += [f32(WORK[level], 128) for level in range(3)] + [f32(6, 128, 128)]
    for level, count, nine in ((0, 1, 1), (0, 2, 0), (1, 2, 0), (0, 2, 1), (0, 2, 0)):
        scratch += exchange_buffers(level, count, nine)
    for count in (1, 2, 2):
        scratch += [f32(count, 2, 8, 128), f32(3, count, 2, 24, 128)]
    scratch += [f32(4, 2, 2, 32, 128), f32(4, 2, 2, 32, 128)]
    scratch += [f32(8, 24, 128), f32(4, 24, 128), f32(4, 24, 128)]
    copies = 6 + 8 * 8 + 3 + 13
    scratch += [pltpu.SemaphoreType.DMA((copies,)), pltpu.SemaphoreType.DMA((copies,))]
    vmem = pl.BlockSpec(memory_space=pltpu.VMEM)
    smem = pl.BlockSpec(memory_space=pltpu.SMEM)
    block = jax.ShapeDtypeStruct(block, jnp.float32)
    return pl.pallas_call(
        kernel,
        out_shape=(block, block, jax.ShapeDtypeStruct((3,), jnp.float32)),
        in_specs=[pl.BlockSpec(memory_space=pl.ANY)] * 4,
        out_specs=(vmem, vmem, smem),
        scratch_shapes=scratch,
        compiler_params=pltpu.CompilerParams(
            collective_id=0, has_side_effects=True, vmem_limit_bytes=48 * 2**20
        ),
    )(source_term, conductivity, jacobi_weights, cotangent)


def solution(mesh):
    return jax.shard_map(
        body,
        mesh=mesh,
        in_specs=(P("gx", "gy", "gz"), P("gx", "gy", "gz"), P(), P("gx", "gy", "gz")),
        out_specs=(P("gx", "gy", "gz"), P("gx", "gy", "gz"), P()),
        check_vma=False,
    )
```

```python
import functools

import jax
import jax.numpy as jnp
from jax import lax
from jax.experimental import pallas as pl
from jax.experimental.pallas import tpu as pltpu
from jax.sharding import PartitionSpec as P

MESH = pl.DeviceIdType.MESH
CELLS = 32 * 128 * 1024
PLANES = (16, 4, 2)
WORK = (48, 32, 24)
ROWS = (64, 48, 40)
GROUP = (64, 32, 32)
OWN = (32, 16, 8)
FIRST = (16, 8, 12)
AROUND = [(ds, dy) for ds in (-1, 0, 1) for dy in (-1, 0, 1) if (ds, dy) != (0, 0)]


def lane_of(rows):
    return lax.broadcasted_iota(jnp.int32, (rows, 128), 1)


def row_of(rows):
    return lax.broadcasted_iota(jnp.int32, (rows, 128), 0)


def roll(values, shift):
    shift = shift % 128
    return values if shift == 0 else pltpu.roll(values, shift, 1)


def kernel(
    f_hbm, c_hbm, w_hbm, g_hbm, sol_ref, grad_ref, wg_ref,
    f_ref, c_ref, g_ref, w_ref, load_sem, pkc, pkf, tbc, tbf, ef, ua, ub, fr, kk, dd, qq, tt, sv,
    c1, ua1, ub1, fr1, kk1, dd1, qq1, tt1, sv1,
    c2, ua2, ub2, fr2, kk2, dd2, qq2, sv2,
    inside0, inside1, inside2, mats,
    *rest,
):
    ex = [rest[6 * i : 6 * i + 6] for i in range(5)]
    rest = rest[30:]
    ga = [rest[2 * i : 2 * i + 2] for i in range(3)]
    po, ob, ra, rb, rc = rest[6:11]
    send_sem, recv_sem = rest[11:13]

    x, y, z = lax.axis_index("gx"), lax.axis_index("gy"), lax.axis_index("gz")
    odd = lax.rem(z, 2)

    def flip(value, parity):
        return value + parity * (3 - 2 * value)

    part = flip(x, odd)
    slab = 4 * z + part

    def peer(ds, dy):
        other = lax.rem(slab + ds + 32, 32)
        oz = lax.div(other, 4)
        ox = flip(lax.rem(other, 4), lax.rem(oz, 2))
        return (ox, lax.rem(y + dy + 4, 4), oz)

    x_peers = [(lax.rem(x + d, 4), y, z) for d in (1, 2, 3)]
    y_peers = [(x, lax.rem(y + d, 4), z) for d in (1, 2, 3)]
    z_peers = [(x, y, lax.rem(z + d, 8)) for d in range(1, 8)]
    peers = {o: peer(*o) for o in AROUND}

    loads = [
        pltpu.make_async_copy(src, dst, load_sem.at[index])
        for index, (src, dst) in enumerate(
            ((c_hbm, c_ref), (f_hbm, f_ref), (g_hbm, g_ref), (w_hbm, w_ref))
        )
    ]
    for load in loads:
        load.start()
    barrier = pltpu.get_barrier_semaphore()
    greeted = x_peers + list(peers.values()) + [y_peers[1]] + z_peers
    for device in greeted:
        pl.semaphore_signal(barrier, inc=1, device_id=device, device_id_type=MESH)

    def remote(src, dst, device, slot):
        copy = pltpu.make_async_remote_copy(
            src_ref=src, dst_ref=dst, send_sem=send_sem.at[slot], recv_sem=recv_sem.at[slot],
            device_id=device, device_id_type=MESH,
        )
        copy.start()
        return copy

    def arrive(copies):
        for copy in copies:
            copy.wait_recv()

    def leave_behind(copies):
        for copy in copies:
            copy.wait_send()

    lane32 = lane_of(32)

    def quarters(ref, out, field):
        for x1 in range(2):
            planes = [ref[4 * x1 + x0] for x0 in range(4)]
            for p in range(4):
                packed = roll(planes[0], -32 * p)
                for x0 in range(1, 4):
                    packed = jnp.where(lane32 // 32 == x0, roll(planes[x0], 32 * (x0 - p)), packed)
                out[p, field, x1] = packed

    def scatter(out, land, slot):
        copies = []
        for d in (1, 2, 3):
            other = lax.rem(x + d, 4)
            copies.append(remote(out.at[flip(other, odd)], land.at[x], (other, y, z), slot + d))
        return copies

    loads[0].wait()
    quarters(c_ref, pkc, 0)
    pl.semaphore_wait(barrier, len(greeted))
    way_c = scatter(pkc, tbc, 31)
    loads[1].wait()
    quarters(f_ref, pkf, 0)
    loads[2].wait()
    quarters(g_ref, pkf, 1)
    way_f = scatter(pkf, tbf, 34)
    loads[3].wait()

    for level, ref in enumerate((inside0, inside1, inside2)):
        rows, lanes = row_of(WORK[level]) - 8, lane_of(WORK[level]) % GROUP[level] - FIRST[level]
        own = OWN[level]
        good = (lanes >= -8) & (lanes < own + 8)
        good &= ((rows >= 0) | (y > 0)) & ((rows < own) | (y < 3))
        good &= ((lanes >= 0) | (slab > 0)) & ((lanes < own) | (slab < 31))
        ref[...] = good.astype(jnp.float32)
    src, dst = row_of(128), lane_of(128)
    for t in range(2):
        mats[t] = jnp.where(dst == (2 * (src // 64) + t) * 32 + (src % 64) // 2, 0.125, 0.0)
        mats[2 + t] = jnp.where(src == (2 * (dst // 64) + t) * 32 + (dst % 64) // 2, 1.0, 0.0)
    mats[4] = jnp.where((dst // 32 == src // 32) & (dst % 32 == 8 + (src % 32) // 2), 0.125, 0.0)
    mats[5] = jnp.where((dst // 32 == src // 32) & (src % 32 == 8 + (dst % 32) // 2), 1.0, 0.0)
    for ref in (c1, ua1, ub1, tt1, c2, ua2, ub2):
        ref[...] = jnp.zeros_like(ref)
    for ref in (tt, ua, ub, ef):
        edge = jnp.zeros(ref.shape[:-2] + (8, 128), jnp.float32)
        ref[..., 0:8, :] = edge
        ref[..., 56:64, :] = edge

    group32 = lane32 // 64

    def build(land, field, to):
        for h in range(2):
            for x1 in range(2):
                low, high = land[h, field, x1], land[2 + h, field, x1]
                for x0 in range(4):
                    plane = jnp.where(group32 == 0, roll(low, 16 - 32 * x0), roll(high, 80 - 32 * x0))
                    ef[to, 1 + 8 * h + 4 * x1 + x0, 16:48] = plane

    def pack(level, ref, bufs, count, nine=False, start=0):
        zs, ys = bufs[:2]
        own, first, group = OWN[level], FIRST[level], GROUP[level]
        per = group // 8
        lanes = lane_of(own) % group
        lanes8 = lane_of(8) % group
        mine = (lanes8 >= first) & (lanes8 < first + own)

        def step(field, unused):
            at = start + field
            ninths = []
            for i in range(PLANES[level] // per):
                left = right = left9 = right9 = None
                for k in range(per):
                    plane = ref[at, 1 + i * per + k, 16 : 16 + own]
                    a, b = roll(plane, 8 * k - first), roll(plane, 8 * k - first - own + 8)
                    left = a if k == 0 else jnp.where(lanes // 8 == k, a, left)
                    right = b if k == 0 else jnp.where(lanes // 8 == k, b, right)
                    if nine:
                        left9 = a if k == 0 else jnp.where(lanes // 8 == (k + 1) % per, a, left9)
                        right9 = b if k == 0 else jnp.where(lanes // 8 == (k - 1) % per, b, right9)
                zs[0, field, i] = left
                zs[1, field, i] = right
                ninths.append((left9, right9))
            if nine:
                zs[0, field, 2] = jnp.where(lanes % 8 < 4, ninths[0][0], roll(ninths[1][0], 4))
                zs[1, field, 2] = jnp.where(lanes % 8 >= 4, ninths[0][1], roll(ninths[1][1], -4))
            for i in range(PLANES[level] // 2):
                for side, row in ((0, 16), (1, 8 + own)):
                    a, b = ref[at, 1 + 2 * i, row : row + 8], ref[at, 2 + 2 * i, row : row + 8]
                    ys[side, field, i] = jnp.where(mine, a, roll(b, group // 2))
                if nine:
                    for side, row in ((0, 24), (1, 39)):
                        a, b = ref[at, 1 + 2 * i, row : row + 1], ref[at, 2 + 2 * i, row : row + 1]
                        ys[side, field, 8, i : i + 1] = jnp.where(mine[:1], a, roll(b, group // 2))
            return unused

        lax.fori_loop(0, count, step, 0)

    def send(level, bufs, slot):
        zs, ys, ls, rs, yl, yh = bufs
        own = OWN[level]
        low, high, face = pl.ds(0, 8), pl.ds(own + 8, 8), pl.ds(8, own)
        first, last = pl.ds(0, 8), pl.ds(own - 8, 8)
        strips = pl.ds(0, PLANES[level] * 8 // GROUP[level])
        return [
            remote(zs.at[1], ls.at[:, :, face], peers[1, 0], slot + 0),
            remote(zs.at[0], rs.at[:, :, face], peers[-1, 0], slot + 1),
            remote(ys.at[1], yl, peers[0, 1], slot + 2),
            remote(ys.at[0], yh, peers[0, -1], slot + 3),
            remote(zs.at[1, :, strips, last], ls.at[:, strips, low], peers[1, 1], slot + 4),
            remote(zs.at[1, :, strips, first], ls.at[:, strips, high], peers[1, -1], slot + 5),
            remote(zs.at[0, :, strips, last], rs.at[:, strips, low], peers[-1, 1], slot + 6),
            remote(zs.at[0, :, strips, first], rs.at[:, strips, high], peers[-1, -1], slot + 7),
        ]

    def ghosts(level, ref, count):
        planes, work, group = PLANES[level], WORK[level], GROUP[level]
        at = slice(8, 8 + work)
        lanes = lane_of(work)
        for field in range(count):
            before, after = ref[field, planes, at], ref[field, 1, at]
            ref[field, 0, at] = jnp.where(lanes < group, 0.0, roll(before, group))
            ref[field, planes + 1, at] = jnp.where(lanes >= 128 - group, 0.0, roll(after, -group))

    insides = (inside0, inside1, inside2)
    has_left, has_right = (slab > 0).astype(jnp.float32), (slab < 31).astype(jnp.float32)
    has_low, has_high = (y > 0).astype(jnp.float32), (y < 3).astype(jnp.float32)

    def unpack(level, ref, bufs, count, nine=False, start=0):
        ls, rs, yl, yh = bufs[2:]
        own, first, group, work = OWN[level], FIRST[level], GROUP[level], WORK[level]
        per = group // 8
        lanes = lane_of(work) % group
        mine = (lanes >= first) & (lanes < first + own)
        before = lanes < first
        lanes9 = lane_of(own) % group

        def step(field, unused):
            at = start + field
            keep = insides[level][...]
            for i in range(PLANES[level] // per):
                left, right = ls[field, i], rs[field, i]
                for k in range(per):
                    plane = i * per + k
                    low, high = yl[field, plane // 2], yh[field, plane // 2]
                    if plane % 2:
                        low, high = roll(low, -(group // 2)), roll(high, -(group // 2))
                    middle = ref[at, 1 + plane, 16 : 16 + own]
                    base = jnp.concatenate([low, middle, high], axis=0)
                    sides = jnp.where(
                        before, roll(left, first - 8 - 8 * k), roll(right, first + own - 8 * k)
                    )
                    ref[at, 1 + plane, 8 : 8 + work] = jnp.where(mine, base, sides) * keep
                    if nine:
                        left9 = roll(ls[field, 2, 8 : 8 + own], 8 + 4 * i - 8 * k) * has_left
                        right9 = roll(rs[field, 2, 8 : 8 + own], 48 - 4 * i - 8 * k) * has_right
                        middle = ref[at, 1 + plane, 16 : 16 + own]
                        middle = jnp.where(lanes9 == 7, left9, middle)
                        middle = jnp.where(lanes9 == 56, right9, middle)
                        ref[at, 1 + plane, 16 : 16 + own] = middle
                        for rows, row, has in ((yl, 7, has_low), (yh, 56, has_high)):
                            ninth = rows[field, 8, plane // 2 : plane // 2 + 1]
                            if plane % 2:
                                ninth = roll(ninth, -(group // 2))
                            ref[at, 1 + plane, row : row + 1] = jnp.where(mine[:1], ninth * has, 0.0)
            return unused

        lax.fori_loop(0, count, step, 0)

    def beside(ref, field, plane, work):
        here = ref[field, plane + 1, 8 : 8 + work]
        return here, [
            ref[field, plane + 2, 8 : 8 + work],
            ref[field, plane, 8 : 8 + work],
            ref[field, plane + 1, 9 : 9 + work],
            ref[field, plane + 1, 7 : 7 + work],
            roll(here, -1),
            roll(here, 1),
        ]

    def setup(level, cells, kref, dref, qref):
        work = WORK[level]
        factor = 0.5 * 0.25**level

        def step(plane, unused):
            here, around = beside(cells, 0, plane, work)
            couplings = [factor * (here + other) for other in around]
            diagonal = couplings[0]
            for coupling in couplings[1:]:
                diagonal = diagonal + coupling
            good = (insides[level][...] > 0.5) & (diagonal > 0.0)
            inverse = jnp.where(good, 1.0 / jnp.where(good, diagonal, 1.0), 0.0)
            for index, coupling in enumerate(couplings):
                kref[index, plane] = inverse * coupling
            dref[plane] = diagonal
            qref[plane] = inverse
            return unused

        lax.fori_loop(0, PLANES[level], step, 0, unroll=True)

    krefs, drefs, frefs, svs = (kk, kk1, kk2), (dd, dd1, dd2), (fr, fr1, fr2), (sv, sv1, sv2)

    def residual(level, ref, field, plane):
        here, around = beside(ref, field, plane, WORK[level])
        total = frefs[level][field, plane] - here
        for index in range(6):
            total = total + krefs[level][index, plane] * around[index]
        return here, total

    def sweep(level, old, new, save=None, fields=(0, 1)):
        weight = w_ref[level]

        def step(plane, unused):
            for field in fields:
                here, r = residual(level, old, field, plane)
                new[field, plane + 1, 8 : 8 + WORK[level]] = here + weight * r
                if save is not None:
                    svs[level][save, field, plane] = r[8 : 8 + OWN[level]]
            return unused

        lax.fori_loop(0, PLANES[level], step, 0, unroll=True)
        if len(fields) == 2:
            ghosts(level, new, 2)

    def first_sweep(level, new):
        weight = w_ref[level]

        def step(plane, unused):
            for field in range(2):
                new[field, plane + 1, 8 : 8 + WORK[level]] = weight * frefs[level][field, plane]
            return unused

        lax.fori_loop(0, PLANES[level], step, 0, unroll=True)
        ghosts(level, new, 2)

    def defect(level, ref, out, save=None):
        work = WORK[level]

        def step(pair, unused):
            for field in range(2):
                total = None
                for side in range(2):
                    plane = 2 * pair + side
                    r = residual(level, ref, field, plane)[1]
                    if save is not None:
                        svs[level][save, field, plane] = r[8 : 8 + OWN[level]]
                    e = drefs[level][plane] * r
                    total = e if total is None else total + e
                out[field, pair, 8 : 8 + work] = total
            return unused

        lax.fori_loop(0, PLANES[level] // 2, step, 0, unroll=True)

    def dot(a, b):
        high = a.astype(jnp.bfloat16)
        rest = a - high.astype(jnp.float32)
        mid = rest.astype(jnp.bfloat16)
        low = (rest - mid.astype(jnp.float32)).astype(jnp.bfloat16)
        b = b.astype(jnp.bfloat16)
        out = jnp.dot(low, b, preferred_element_type=jnp.float32)
        out = out + jnp.dot(mid, b, preferred_element_type=jnp.float32)
        return out + jnp.dot(high, b, preferred_element_type=jnp.float32)

    def pairs(ref, field, plane, rows):
        even = ref[field, plane, pl.ds(0, rows // 2, stride=2), :]
        return even + ref[field, plane, pl.ds(1, rows // 2, stride=2), :]

    def restricted(level, ref, field):
        if level == 0:
            a = jnp.concatenate([pairs(ref, field, m, 64) for m in range(4)], axis=0)
            b = jnp.concatenate([pairs(ref, field, 4 + m, 64) for m in range(4)], axis=0)
            return (dot(a, mats[0]) + dot(b, mats[1])).reshape(4, 32, 128)
        a = jnp.concatenate([pairs(ref, field, m, 48) for m in range(2)], axis=0)
        return dot(a, mats[4]).reshape(2, 24, 128)

    def prolong(level, ref, out):
        for field in range(2):
            if level == 0:
                w = ref[field, 1:5, 8:40].reshape(128, 128)
                for t in range(2):
                    moved = dot(w, mats[2 + t]).reshape(4, 32, 128)
                    for m in range(4):
                        out[field, 4 * t + m, pl.ds(0, 32, stride=2), :] = moved[m]
                        out[field, 4 * t + m, pl.ds(1, 32, stride=2), :] = moved[m]
            else:
                w = ref[field, 1:3, 8:32].reshape(48, 128)
                moved = dot(w, mats[5]).reshape(2, 24, 128)
                for m in range(2):
                    out[field, m, pl.ds(0, 24, stride=2), :] = moved[m]
                    out[field, m, pl.ds(1, 24, stride=2), :] = moved[m]

    def product(level, a, b, fa, fb):
        own, first = OWN[level], FIRST[level]
        lanes = lane_of(own) % GROUP[level]
        mine = (lanes >= first) & (lanes < first + own)

        def step(plane, total):
            saved = svs[level]
            value = drefs[level][plane, 8 : 8 + own] * saved[a, fa, plane] * saved[b, fb, plane]
            value = jnp.where(mine, value, 0.0)
            for tile in range(own // 8):
                total = total + value[8 * tile : 8 * tile + 8]
            return total

        return lax.fori_loop(0, PLANES[level], step, jnp.zeros((8, 128), jnp.float32))

    def gather(bufs, slot):
        own, land = bufs
        return [
            remote(own, land.at[1 - ds, :, :, pl.ds(8 - 8 * dy, 8)], peers[ds, dy], slot + index)
            for index, (ds, dy) in enumerate(AROUND)
        ]

    lanes2 = lane_of(24) % 32

    def gathered(land, field, plane):
        sides = jnp.where(
            lanes2 < 12, roll(land[0, field, plane], -8), roll(land[2, field, plane], 8)
        )
        mine = (lanes2 >= 12) & (lanes2 < 20)
        return jnp.where(mine, land[1, field, plane], sides) * inside2[...]

    tbc[x] = pkc[part]
    arrive(way_c)
    build(tbc, 0, 0)
    pack(0, ef, ex[0], 1, True)
    halo_c = send(0, ex[0], 0)
    leave_behind(way_c)
    tbf[x] = pkf[part]
    arrive(way_f)
    for field in range(2):
        build(tbf, field, 1 + field)
    pack(0, ef, ex[1], 2, start=1)
    halo_f = send(0, ex[1], 8)
    leave_behind(way_f)

    def add_planes(pair, unused):
        tt[0, pair, 16:48] = ef[0, 1 + 2 * pair, 16:48] + ef[0, 2 + 2 * pair, 16:48]
        return unused

    lax.fori_loop(0, 8, add_planes, 0)
    early = restricted(0, tt, 0)
    for pair in range(2):
        tt1[0, pair, 8:40] = early[2 * pair] + early[2 * pair + 1]
    early = restricted(1, tt1, 0)
    own2, land2 = ga[0]
    for plane in range(2):
        own2[0, plane] = early[plane, 8:16]
        land2[1, 0, plane, 8:16] = early[plane, 8:16]
    coarse_copies = gather(ga[0], 16)
    leave_behind(halo_c)

    arrive(halo_c)
    unpack(0, ef, ex[0], 1, True)
    ghosts(0, ef, 1)
    setup(0, ef, kk, dd, qq)

    def add_planes_whole(pair, unused):
        tt[0, pair, 8:56] = ef[0, 1 + 2 * pair, 8:56] + ef[0, 2 + 2 * pair, 8:56]
        return unused

    lax.fori_loop(0, 8, add_planes_whole, 0)
    cells = restricted(0, tt, 0)
    for plane in range(4):
        c1[0, plane + 1, 8:40] = cells[plane] * inside1[...]
    ghosts(1, c1, 1)
    setup(1, c1, kk1, dd1, qq1)
    arrive(coarse_copies)
    for plane in range(2):
        c2[0, plane + 1, 8:32] = gathered(land2, 0, plane)
    ghosts(2, c2, 1)
    setup(2, c2, kk2, dd2, qq2)

    leave_behind(coarse_copies + halo_f)
    arrive(halo_f)
    unpack(0, ef, ex[1], 2, start=1)

    def right_side(plane, unused):
        for field in range(2):
            fr[field, plane] = qq[plane] * ef[1 + field, plane + 1, 8:56]
        return unused

    lax.fori_loop(0, 16, right_side, 0)

    first_sweep(0, ua)
    sweep(0, ua, ub, 0)
    defect(0, ub, tt, 3)

    def coarse_right_side(level, source, fine):
        for field in range(2):
            values = restricted(level, fine, field)
            for plane in range(PLANES[level + 1]):
                source(field, plane, values[plane])

    def keep1(field, plane, value):
        fr1[field, plane] = value

    coarse_right_side(0, keep1, tt)

    def scale1():
        for field in range(2):
            for plane in range(4):
                fr1[field, plane] = qq1[plane] * fr1[field, plane]

    def middle(cycle, before):
        first_sweep(1, ua1)
        sweep(1, ua1, ub1, 2 * cycle)
        defect(1, ub1, tt1)
        own, land = ga[1 + cycle]

        def keep2(field, plane, value):
            scaled = qq2[plane, 8:16] * value[8:16]
            own[field, plane] = scaled
            land[1, field, plane, 8:16] = scaled

        coarse_right_side(1, keep2, tt1)
        copies = gather(ga[1 + cycle], (24, 8)[cycle])
        if cycle == 1:
            pack(1, ub1, ex[2], 2)
            more = send(1, ex[2], 16)
        leave_behind(before)
        arrive(copies)
        for field in range(2):
            for plane in range(2):
                fr2[field, plane] = gathered(land, field, plane)
        first_sweep(2, ua2)
        refs = (ua2, ub2)
        for index in range(1, 8):
            save = cycle if index == 3 + cycle else None
            sweep(2, refs[(index + 1) % 2], refs[index % 2], save)
        prolong(1, ub2, tt1)
        if cycle == 1:
            arrive(more)
            unpack(1, ub1, ex[2], 2)
        for field in range(2):
            for plane in range(4):
                ub1[field, plane + 1, 8:40] = (
                    ub1[field, plane + 1, 8:40] + tt1[field, plane // 2, 8:40]
                )
        ghosts(1, ub1, 2)
        sweep(1, ub1, ua1, 1 + 2 * cycle)
        sweep(1, ua1, ub1)
        return copies + more if cycle == 1 else copies

    def correct(ref):
        prolong(0, ub1, tt)

        def step(plane, unused):
            for field in range(2):
                ref[field, plane + 1, 16:48] = (
                    ref[field, plane + 1, 16:48] + tt[field, lax.div(plane, 2), 16:48]
                )
            return unused

        lax.fori_loop(0, 16, step, 0, unroll=4)

    scale1()
    sent = middle(0, [])
    correct(ub)
    pack(0, ub, ex[3], 2, True)
    fine = send(0, ex[3], 0)
    leave_behind(sent)
    arrive(fine)
    unpack(0, ub, ex[3], 2, True)
    ghosts(0, ub, 2)
    sweep(0, ub, ua)
    sweep(0, ua, ub, 1)
    sweep(0, ub, ua, 2)
    sweep(0, ua, ub)
    defect(0, ub, tt, 4)
    coarse_right_side(0, keep1, tt)
    scale1()
    sent = middle(1, fine)
    correct(ub)
    pack(0, ub, ex[4], 2)
    copies = send(0, ex[4], 24)

    own_lanes = (lane32 % 64 >= 16) & (lane32 % 64 < 48)

    def corrected(plane, total):
        value = None
        for field in range(2):
            change = sv[0, 1 - field, plane] - sv[3, 1 - field, plane]
            term = change * tt[field, lax.div(plane, 2), 16:48]
            value = term if value is None else value + term
        value = jnp.where(own_lanes, value * dd[plane, 8:40], 0.0)
        return total + ((value[0:8] + value[8:16]) + (value[16:24] + value[24:32]))

    moved = lax.fori_loop(0, 16, corrected, jnp.zeros((8, 128), jnp.float32), unroll=4)
    scale = 1.0 / CELLS
    sums = [
        2.0 * (product(0, 0, 4, 0, 1) + product(0, 4, 0, 0, 1) - moved * (1.0 / w_ref[0]))
        + 4.0 * product(0, 1, 2, 0, 1),
        16.0
        * (
            product(1, 0, 3, 0, 1)
            + product(1, 3, 0, 0, 1)
            + product(1, 1, 2, 0, 1)
            + product(1, 2, 1, 0, 1)
        ),
        512.0 * (product(2, 0, 1, 0, 1) + product(2, 1, 0, 0, 1)),
    ]
    for level in range(3):
        ra[z, 8 * level : 8 * level + 8] = sums[level] * scale
    copies_a = [remote(ra.at[z], ra.at[z], device, 38 + i) for i, device in enumerate(z_peers)]
    leave_behind(sent)

    arrive(copies)
    unpack(0, ub, ex[4], 2)
    ghosts(0, ub, 2)
    sweep(0, ub, ua)
    arrive(copies_a)
    total = ra[0]
    for index in range(1, 8):
        total = total + ra[index]
    rb[y] = total
    copies_b = [remote(rb.at[y], rb.at[y], device, 45 + i) for i, device in enumerate(y_peers)]
    leave_behind(copies + copies_a)
    copies_o = []
    for field in range(2):
        sweep(0, ua, ub, None, (field,))
        for h in range(2):
            for x1 in range(2):
                planes = [ub[field, 1 + 8 * h + 4 * x1 + x0, 16:48] for x0 in range(4)]
                for g in range(2):
                    packed = roll(planes[0], -64 * g - 16)
                    for x0 in range(1, 4):
                        packed = jnp.where(
                            lane32 // 32 == x0, roll(planes[x0], 32 * x0 - 64 * g - 16), packed
                        )
                    po[field, 2 * g + h, x1] = packed
        sent = []
        for d in (1, 2, 3):
            other = lax.rem(x + d, 4)
            sent.append(
                remote(po.at[field, other], ob.at[field, part], (other, y, z), 50 + 3 * field + d)
            )
        copies_o.append(sent)
        ob[field, part] = po[field, x]

    arrive(copies_b)
    total = rb[0]
    for index in range(1, 4):
        total = total + rb[index]
    rc[x] = total
    copies_c = [remote(rc.at[x], rc.at[x], device, 48 + i) for i, device in enumerate(x_peers)]
    leave_behind(copies_b)

    for field, ref in enumerate((sol_ref, grad_ref)):
        arrive(copies_o[field])
        for x1 in range(2):
            parts = [ob[field, p, x1] for p in range(4)]
            for x0 in range(4):
                out = roll(parts[0], -32 * x0)
                for p in range(1, 4):
                    out = jnp.where(lane32 // 32 == p, roll(parts[p], 32 * (p - x0)), out)
                ref[4 * x1 + x0] = out

    arrive(copies_c)
    total = rc[0]
    for index in range(1, 4):
        total = total + rc[index]
    for level in range(3):
        wg_ref[level] = jnp.sum(total[8 * level : 8 * level + 8])
    leave_behind(copies_c + copies_o[0] + copies_o[1])


def f32(*shape):
    return pltpu.VMEM(shape, jnp.float32)


def exchange_buffers(level, count, nine):
    own, strips, half = OWN[level], PLANES[level] * 8 // GROUP[level] + nine, PLANES[level] // 2 + nine
    return [
        f32(2, count, strips, own, 128),
        f32(2, count, half, 8, 128),
        f32(count, strips, own + 16, 128),
        f32(count, strips, own + 16, 128),
        f32(count, half, 8, 128),
        f32(count, half, 8, 128),
    ]


def level_buffers(level):
    planes, work, rows, own = PLANES[level], WORK[level], ROWS[level], OWN[level]
    out = [
        f32(2, planes + 2, rows, 128),
        f32(2, planes + 2, rows, 128),
        f32(2, planes, work, 128),
        f32(6, planes, work, 128),
        f32(planes, work, 128),
        f32(planes, work, 128),
    ]
    if level < 2:
        out.append(f32(2, planes // 2, rows, 128))
    out.append(f32((5, 4, 2)[level], 2, planes, own, 128))
    return out


def body(source_term, conductivity, jacobi_weights, cotangent):
    block = source_term.shape
    scratch = [f32(*block), f32(*block), f32(*block), pltpu.SMEM((3,), jnp.float32)]
    scratch += [pltpu.SemaphoreType.DMA((4,))]
    scratch += [f32(4, count, 2, 32, 128) for count in (1, 2, 1, 2)] + [f32(3, 18, 64, 128)]
    scratch += level_buffers(0)
    scratch += [f32(1, 6, 48, 128)] + level_buffers(1)
    scratch += [f32(1, 4, 40, 128)] + level_buffers(2)
    scratch += [f32(WORK[level], 128) for level in range(3)] + [f32(6, 128, 128)]
    for level, count, nine in ((0, 1, 1), (0, 2, 0), (1, 2, 0), (0, 2, 1), (0, 2, 0)):
        scratch += exchange_buffers(level, count, nine)
    for count in (1, 2, 2):
        scratch += [f32(count, 2, 8, 128), f32(3, count, 2, 24, 128)]
    scratch += [f32(2, 4, 2, 32, 128), f32(2, 4, 2, 32, 128)]
    scratch += [f32(8, 24, 128), f32(4, 24, 128), f32(4, 24, 128)]
    copies = 57
    scratch += [pltpu.SemaphoreType.DMA((copies,)), pltpu.SemaphoreType.DMA((copies,))]
    vmem = pl.BlockSpec(memory_space=pltpu.VMEM)
    smem = pl.BlockSpec(memory_space=pltpu.SMEM)
    block = jax.ShapeDtypeStruct(block, jnp.float32)
    return pl.pallas_call(
        kernel,
        out_shape=(block, block, jax.ShapeDtypeStruct((3,), jnp.float32)),
        in_specs=[pl.BlockSpec(memory_space=pltpu.HBM)] * 4,
        out_specs=(vmem, vmem, smem),
        scratch_shapes=scratch,
        compiler_params=pltpu.CompilerParams(
            collective_id=0, has_side_effects=True, vmem_limit_bytes=62 * 2**20
        ),
    )(source_term, conductivity, jacobi_weights, cotangent)


def solution(mesh):
    return jax.shard_map(
        body,
        mesh=mesh,
        in_specs=(P("gx", "gy", "gz"), P("gx", "gy", "gz"), P(), P("gx", "gy", "gz")),
        out_specs=(P("gx", "gy", "gz"), P("gx", "gy", "gz"), P()),
        check_vma=False,
    )
```
